256 devices in a mesh: dp: 32 (over x_lo, z, core), tp: 8 (over y, x_hi).
Axes of the slice: x: 4 (x_hi: 2, x_lo: 2; x = x_hi * 2 + x_lo), y: 4, z: 8, core: 2. Of those that a mesh axis runs over, the one named last changes fastest.
Arguments:
- gate_param: bfloat16 [4096, 14336], P(('dp', 'tp')), may hold values from -4 to 4
- up_param: bfloat16 [4096, 14336], P(('dp', 'tp')), may hold values from -4 to 4
- gate_grad: bfloat16 [4096, 14336], P(('dp', 'tp')), may hold values from -6 to 6
- up_grad: bfloat16 [4096, 14336], P(('dp', 'tp')), may hold values from -6 to 6
- gate_mom: bfloat16 [4096, 14336], P(('dp', 'tp')), may hold values from -2 to 2
- up_mom: bfloat16 [4096, 14336], P(('dp', 'tp')), may hold values from -2 to 2
- gate_var: bfloat16 [4096, 14336], P(('dp', 'tp')), may hold values from 0.049804688 to 1
- up_var: bfloat16 [4096, 14336], P(('dp', 'tp')), may hold values from 0.049804688 to 1
- queries: bfloat16 [1024, 2, 4096], P('dp', None, 'tp'), may hold values from -20 to 20
- new_keys: bfloat16 [1024, 2, 1024], P('dp', None, 'tp'), may hold values from -6 to 6
- new_values: bfloat16 [1024, 2, 1024], P('dp', None, 'tp'), may hold values from -6 to 6
- cache_keys: bfloat16 [1024, 192, 1024], P('dp', None, 'tp'), may hold values from -6 to 6
- cache_values: bfloat16 [1024, 192, 1024], P('dp', None, 'tp'), may hold values from -6 to 6
- cache_len: int32 [1024], P('dp'), may hold values from 2 to 192, as said below
- residual: bfloat16 [1024, 2, 4096], P('dp', None, 'tp'), may hold values from -180 to 180
- out_proj: bfloat16 [4096, 4096], P('tp'), may hold values from -0.09375 to 0.09375
- norm_gain: bfloat16 [4096], replicated, may hold values from 0.099609375 to 1.8984375
Outputs:
- gate_updated: bfloat16 [4096, 14336], P(('dp', 'tp'))
- up_updated: bfloat16 [4096, 14336], P(('dp', 'tp'))
- mixed_stream: bfloat16 [1024, 2, 4096], P('dp', None, 'tp')
- hidden: bfloat16 [1024, 2, 14336], P('dp', None, 'tp')
The draws below stay inside these ranges and needn't reach their ends.
Inputs may be any that keep to these rules, and one draw needn't show every extreme that they name: `cache_len`: each group of 32 rows has a row with exactly 192 filled slots.
All inputs are finite; a program needn't handle non-finite values.
Results may differ from the reference program's by a relative error of at most 0.0082.
Values may be sent and summed in bfloat16 or wider, within the bound.
A program may use at most 128 MiB of HBM per device.

```python
import math
import jax
import jax.numpy as jnp
from jax import lax

D = 4096
FF = 14336
HQ = 32
KVH = 8
HD = 128
ROW_GRP = 32
LEN = 192
ROWS = 1024


def draw_queries(key, part):
    key = jax.random.fold_in(key, 1)
    base = jnp.clip(jax.random.normal(key, (ROWS, 2, HQ * HD), jnp.float32), -6.0, 6.0)
    return base.astype(jnp.bfloat16)


def draw_cache_keys(key, part):
    key = jax.random.fold_in(key, 2)
    base = jnp.clip(jax.random.normal(key, (ROWS, LEN, KVH * HD), jnp.float32), -6.0, 6.0)
    return base.astype(jnp.bfloat16)


def draw_residual(key, part):
    key = jax.random.fold_in(key, 3)
    ramp = 1.0 + 2.0 * jnp.arange(D, dtype=jnp.float32) / D
    base = jnp.clip(jax.random.normal(key, (ROWS, 2, D), jnp.float32), -6.0, 6.0) * ramp
    return base.astype(jnp.bfloat16)


def draw_cache_len(key, part):
    key = jax.random.fold_in(key, 7)
    groups = ROWS // ROW_GRP
    lengths = jax.random.randint(key, (groups, ROW_GRP), 2, LEN + 1)
    fullest = jax.random.randint(jax.random.fold_in(key, 1), (groups,), 0, ROW_GRP)
    column = jnp.arange(ROW_GRP, dtype=jnp.int32)[None, :]
    lengths = jnp.where(column == fullest[:, None], LEN, lengths)
    return lengths.reshape(ROWS).astype(jnp.int32)


def shard_levels(key, shape, cuts, low, largest):
    def one(dim, blocks):
        heights = jax.random.uniform(jax.random.fold_in(jax.random.fold_in(key, 6), dim), (blocks,), jnp.float32, low / len(cuts), largest / len(cuts))
        return jnp.repeat(jnp.exp(heights), shape[dim] // blocks).reshape((-1,) + (1,) * (len(shape) - dim - 1))

    level = one(*cuts[0])
    for cut in cuts[1:]:
        level = level * one(*cut)
    return level


def centred(key, shape, scale, limit, shards=(), held_as=jnp.bfloat16):
    values = jax.random.normal(key, shape, jnp.float32) * scale
    if len(shards) > 0:
        values = shard_levels(key, shape, shards, -0.22, 0.18) * values
    return jnp.clip(values, min=-limit, max=limit).astype(held_as)


def setup_inputs(seed: int = 0) -> dict:
    key_list = jax.random.split(jax.random.key(seed), 18)
    gate_param = centred(key_list[0], (D, FF), 1.0, 4.0, ((0, 256),))
    up_param = centred(key_list[1], (D, FF), 1.0, 4.0, ((0, 256),))
    gate_grad = centred(key_list[2], (D, FF), 1.0, 6.0, ((0, 256),))
    up_grad = centred(key_list[3], (D, FF), 1.0, 6.0, ((0, 256),))
    gate_mom = centred(key_list[4], (D, FF), 0.3, 2.0, ((0, 256),))
    up_mom = centred(key_list[5], (D, FF), 0.3, 2.0, ((0, 256),))
    gate_var = jnp.clip(jnp.exp(math.log(1.0) - 2.9996462 * jax.random.uniform(key_list[6], (D, FF), jnp.float32) ** shard_levels(key_list[6], (D, FF), ((0, 256),), -0.2, 0.2)), 0.049804688, 1.0).astype(jnp.bfloat16)
    up_var = jnp.clip(jnp.exp(math.log(1.0) - 2.9996462 * jax.random.uniform(key_list[7], (D, FF), jnp.float32) ** shard_levels(key_list[7], (D, FF), ((0, 256),), -0.2, 0.2)), 0.049804688, 1.0).astype(jnp.bfloat16)
    queries = draw_queries(jax.random.fold_in(key_list[17], 71), 0)
    new_keys = centred(key_list[9], (ROWS, 2, KVH * HD), 1.0, 6.0, ((0, 32), (2, 8)))
    new_values = centred(key_list[10], (ROWS, 2, KVH * HD), 1.0, 6.0, ((0, 32), (2, 8)))
    cache_keys = draw_cache_keys(jax.random.fold_in(key_list[17], 71), 0)
    cache_values = centred(key_list[12], (ROWS, LEN, KVH * HD), 1.0, 6.0, ((0, 32), (2, 8)))
    cache_len = draw_cache_len(jax.random.fold_in(key_list[17], 71), 0)
    residual = draw_residual(jax.random.fold_in(key_list[17], 71), 0)
    out_proj = centred(key_list[15], (HQ * HD, D), (HQ * HD) ** -0.5, 0.09375, ((0, 8),))
    norm_gain = jnp.clip(1.0 + 0.18 * jax.random.normal(key_list[16], (D,), jnp.float32), 0.099609375, 1.8984375).astype(jnp.bfloat16)
    return {"gate_param": gate_param, "up_param": up_param, "gate_grad": gate_grad, "up_grad": up_grad, "gate_mom": gate_mom, "up_mom": up_mom, "gate_var": gate_var, "up_var": up_var, "queries": queries, "new_keys": new_keys, "new_values": new_values, "cache_keys": cache_keys, "cache_values": cache_values, "cache_len": cache_len, "residual": residual, "out_proj": out_proj, "norm_gain": norm_gain}


beta_one = 0.9
beta_two = 0.95
adam_step = 20
learn_rate = 0.1
decay_rate = 0.1
epsilon_adam = 1e-08
epsilon_norm = 1e-05
masked_score = -1e+30

def adamw_update(param, grad, moment, second):
    grad32 = grad.astype(jnp.float32)
    moment_new = beta_one * moment.astype(jnp.float32) + (1.0 - beta_one) * grad32
    second_new = beta_two * second.astype(jnp.float32) + (1.0 - beta_two) * grad32 * grad32
    corr_one = 1.0 - beta_one ** adam_step
    corr_two = 1.0 - beta_two ** adam_step
    direction = moment_new / corr_one / (jnp.sqrt(second_new / corr_two) + epsilon_adam)
    param32 = param.astype(jnp.float32)
    return (param32 - learn_rate * (direction + decay_rate * param32)).astype(jnp.bfloat16)

def attention(queries, new_keys, new_values, cache_keys, cache_values, cache_len):
    batch_rows = queries.shape[0]
    query_width = queries.shape[2]
    kv_heads = new_keys.shape[2] // HD
    groups = query_width // HD // kv_heads
    slots = cache_keys.shape[1]
    query_heads = queries.reshape(batch_rows, 2, kv_heads, groups, HD).astype(jnp.float32)
    keys_cache = cache_keys.reshape(batch_rows, slots, kv_heads, HD).astype(jnp.float32)
    vals_cache = cache_values.reshape(batch_rows, slots, kv_heads, HD).astype(jnp.float32)
    keys_fresh = new_keys.reshape(batch_rows, 2, kv_heads, HD).astype(jnp.float32)
    vals_fresh = new_values.reshape(batch_rows, 2, kv_heads, HD).astype(jnp.float32)
    scale = 1.0 / math.sqrt(HD)
    score_cache = jnp.einsum('rskgd,rtkd->rskgt', query_heads, keys_cache) * scale
    score_fresh = jnp.einsum('rskgd,rukd->rskgu', query_heads, keys_fresh) * scale
    valid_cache = jnp.arange(slots, dtype=jnp.int32)[None, :] < cache_len[:, None]
    valid_fresh = jnp.arange(2, dtype=jnp.int32)[None, :] <= jnp.arange(2, dtype=jnp.int32)[:, None]
    score_cache = jnp.where(valid_cache[:, None, None, None, :], score_cache, masked_score)
    score_fresh = jnp.where(valid_fresh[None, :, None, None, :], score_fresh, masked_score)
    scores = jnp.concatenate([score_cache, score_fresh], axis=-1)
    top = lax.optimization_barrier(jnp.max(scores, axis=-1, keepdims=True))
    expo = jnp.exp(scores - top)
    weights = (expo / lax.optimization_barrier(jnp.sum(expo, axis=-1, keepdims=True))).astype(jnp.bfloat16).astype(jnp.float32)
    context = jnp.einsum('rskgt,rtkd->rskgd', weights[..., :slots], vals_cache)
    context = context + jnp.einsum('rskgu,rukd->rskgd', weights[..., slots:], vals_fresh)
    return context.reshape(batch_rows, 2, query_width).astype(jnp.bfloat16)

def rms_norm(mixed, gain):
    mixed32 = mixed.astype(jnp.float32)
    factor = lax.rsqrt(lax.optimization_barrier(jnp.mean(mixed32 * mixed32, axis=-1, keepdims=True)) + epsilon_norm)
    return (mixed32 * factor * gain.astype(jnp.float32)).astype(jnp.bfloat16)

def reference(gate_param, up_param, gate_grad, up_grad, gate_mom, up_mom, gate_var, up_var, queries, new_keys, new_values, cache_keys, cache_values, cache_len, residual, out_proj, norm_gain):
    gate_updated = adamw_update(gate_param, gate_grad, gate_mom, gate_var)
    up_updated = adamw_update(up_param, up_grad, up_mom, up_var)
    context = attention(queries, new_keys, new_values, cache_keys, cache_values, cache_len)
    batch_rows = context.shape[0]
    flat = context.reshape(batch_rows * 2, context.shape[2])
    attn_out = jnp.dot(flat, out_proj, preferred_element_type=jnp.float32)
    mixed = (residual.reshape(batch_rows * 2, D).astype(jnp.float32) + attn_out).astype(jnp.bfloat16)
    normed = rms_norm(mixed, norm_gain)
    scale_in = 1.0 / math.sqrt(D)
    gate_act = jnp.dot(normed, gate_updated, preferred_element_type=jnp.float32) * scale_in
    up_act = jnp.dot(normed, up_updated, preferred_element_type=jnp.float32) * scale_in
    hidden = (jax.nn.silu(gate_act) * up_act).astype(jnp.bfloat16)
    return (gate_updated, up_updated, mixed.reshape(batch_rows, 2, D), hidden.reshape(batch_rows, 2, FF))
```

```python
import functools
import math

import jax
import jax.numpy as jnp
from jax import lax
from jax.experimental import pallas as pl
from jax.experimental.pallas import tpu as pltpu
from jax.sharding import PartitionSpec as P

MESH = pl.DeviceIdType.MESH
F32 = jnp.float32
BF16 = jnp.bfloat16

HD = 128
ROWS = 32
SLOTS = 192
PADDED = 208
D = 4096
FF = 14336
NZ, NY = 8, 4
PLANE = NZ * NY
WIDTHS = (512, 384)
PAIR = 896

beta_one = 0.9
beta_two = 0.95
adam_step = 20
learn_rate = 0.1
decay_rate = 0.1
epsilon_adam = 1e-08
epsilon_norm = 1e-05
masked_score = -1e30


def adamw_update(param, grad, moment, second):
    grad32 = grad.astype(F32)
    moment_new = beta_one * moment.astype(F32) + (1.0 - beta_one) * grad32
    second_new = beta_two * second.astype(F32) + (1.0 - beta_two) * grad32 * grad32
    corr_one = 1.0 - beta_one**adam_step
    corr_two = 1.0 - beta_two**adam_step
    direction = moment_new * (1.0 / corr_one) / (
        jnp.sqrt(second_new * (1.0 / corr_two)) + epsilon_adam
    )
    param32 = param.astype(F32)
    return param32 - learn_rate * (direction + decay_rate * param32)


def kernel(
    gp, up, gg, ug, gm, um, gv, uv,
    q_in, nk_in, nv_in, ck_in, cv_in, len_in, res_in, wo_in, gain_in,
    g_out, u_out, mix_out, hid_out,
    adam, gnew, unew, sbuf0, sbuf1, wbuf0, wbuf1,
    qbuf, kbuf, vbuf, lens, res, wo, gain,
    ctx32, ctxb, pbuf, rsbuf, rres, ybuf, mixb, abuf, hbuf, obuf, hfin,
    load_sem, send_sem, a2a_sem, x1_sem, x2_sem, core_sem,
    rs_sem, res_sem, y_sem, zr_sem, mix_sem, out_sem, store_sem,
):
    dp = lax.axis_index("dp")
    tp = lax.axis_index("tp")
    x_lo = dp // 16
    z = (dp // 2) % NZ
    c = dp % 2
    y = tp // 2
    h = tp % 2
    x = h * 2 + x_lo
    other = 1 - h

    def place(xx, yy, zz, cc):
        return ((xx % 2) * 16 + zz * 2 + cc, yy * 2 + xx // 2)

    right = (x + 1) % 4
    left = (x + 3) % 4
    across = (x + 2) % 4
    z_up = (z + 1) % NZ
    z_dn = (z + NZ - 1) % NZ

    loads = []
    for i, ref in enumerate((gp, gg, gm, gv, up, ug, um, uv)):
        loads.append(pltpu.make_async_copy(ref, adam.at[i], load_sem.at[i]))
    load_q = pltpu.make_async_copy(q_in, qbuf, load_sem.at[8])
    load_k = pltpu.make_async_copy(ck_in, kbuf.at[:, pl.ds(0, SLOTS), :], load_sem.at[9])
    load_nk = pltpu.make_async_copy(nk_in, kbuf.at[:, pl.ds(SLOTS, 16), :], load_sem.at[10])
    load_v = pltpu.make_async_copy(cv_in, vbuf.at[:, pl.ds(0, SLOTS), :], load_sem.at[11])
    load_nv = pltpu.make_async_copy(nv_in, vbuf.at[:, pl.ds(SLOTS, 16), :], load_sem.at[12])
    load_len = pltpu.make_async_copy(len_in, lens, load_sem.at[13])
    load_res = pltpu.make_async_copy(res_in, res, load_sem.at[14])
    load_wo = pltpu.make_async_copy(wo_in, wo, load_sem.at[15])
    load_gain = pltpu.make_async_copy(gain_in, gain, load_sem.at[16])
    for copy in loads:
        copy.start()
    for copy in (load_res, load_q, load_k, load_nk, load_len, load_v, load_nv, load_wo, load_gain):
        copy.start()

    barrier = pltpu.get_barrier_semaphore()

    def greet(where):
        pl.semaphore_signal(barrier, inc=1, device_id=where, device_id_type=MESH)

    @pl.loop(1, PLANE)
    def _(o):
        greet(place(x, (y + o // NZ) % NY, (z + o % NZ) % NZ, c))

    @pl.loop(1, NZ)
    def _(o):
        greet(place(across, y, (z + o) % NZ, c))

    @pl.loop(0, NY)
    def _(o):
        greet(place(across, (y + o) % NY, z, c))

    greet(place(right, y, z, c))
    greet(place(left, y, z, c))
    greet(place(x, y, z, 1 - c))

    for copy in loads:
        copy.wait()
    lane16 = lax.broadcasted_iota(jnp.int32, (16, 128), 1)

    @pl.loop(0, 16)
    def _(pair):
        cols = pl.ds(pl.multiple_of(pair * PAIR, 128), PAIR)
        new = []
        for first, dest in ((0, gnew), (4, unew)):
            value = adamw_update(
                adam[first, :, cols],
                adam[first + 1, :, cols],
                adam[first + 2, :, cols],
                adam[first + 3, :, cols],
            )
            dest[:, cols] = value.astype(BF16)
            new.append(value)
        gate = [new[0][:, i * 128 : (i + 1) * 128] for i in range(7)]
        upper = [new[1][:, i * 128 : (i + 1) * 128] for i in range(7)]
        turned = pltpu.roll(upper[3], 64, 1)
        mixed_even = jnp.where(lane16 < 64, gate[3], turned)
        mixed_odd = jnp.where(lane16 < 64, turned, gate[3])
        for half, (a, b, d, middle) in enumerate(((0, 1, 2, mixed_even), (4, 5, 6, mixed_odd))):
            for i, tile in enumerate((gate[a], upper[a], gate[b], upper[b])):
                sbuf0[2 * pair + half, :, i * 128 : (i + 1) * 128] = tile.astype(BF16)
            for i, tile in enumerate((gate[d], upper[d], middle)):
                sbuf1[2 * pair + half, :, i * 128 : (i + 1) * 128] = tile.astype(BF16)

    store_g = pltpu.make_async_copy(gnew, g_out, store_sem.at[0])
    store_u = pltpu.make_async_copy(unew, u_out, store_sem.at[1])
    store_g.start()
    store_u.start()

    pl.semaphore_wait(barrier, PLANE - 1 + NZ - 1 + NY + 3)

    sbufs = (sbuf0, sbuf1)
    wbufs = (wbuf0, wbuf1)

    def remote(src, dst, send, recv, where):
        return pltpu.make_async_remote_copy(
            src_ref=src,
            dst_ref=dst,
            send_sem=send,
            recv_sem=recv,
            device_id=where,
            device_id_type=MESH,
        )

    for q in range(2):
        @pl.loop(1, PLANE)
        def _(o, q=q):
            yy = (y + o // NZ) % NY
            zz = (z + o % NZ) % NZ
            remote(
                sbufs[q].at[yy * NZ + zz],
                wbufs[q].at[x_lo, z, c, y, h],
                send_sem.at[q],
                a2a_sem.at[q],
                place(x, yy, zz, c),
            ).start()

        wbufs[q][x_lo, z, c, y, h] = sbufs[q][y * NZ + z]

    load_res.wait()
    to_across = place(across, y, z, c)
    res_copy = remote(res.at[other], rres.at[h], send_sem.at[2], res_sem, to_across)
    res_copy.start()
    rres[h] = res[h]

    for copy in (load_q, load_k, load_nk, load_len, load_v, load_nv):
        copy.wait()
    part = 8

    @pl.loop(0, ROWS // part)
    def _(i):
        rows = pl.ds(pl.multiple_of(i * part, part), part)
        slot = lax.broadcasted_iota(jnp.int32, (part, 8, PADDED), 2)
        token = lax.broadcasted_iota(jnp.int32, (part, 8, PADDED), 1) // 4
        scores = lax.dot_general(
            qbuf[rows], kbuf[rows], (((2,), (2,)), ((0,), (0,))), preferred_element_type=F32
        ) * (1.0 / math.sqrt(HD))
        filled = lens[rows][:, :, 0:1]
        fresh = (slot >= SLOTS) & (slot <= SLOTS + token)
        scores = jnp.where((slot < filled) | fresh, scores, masked_score)
        expo = jnp.exp(scores - jnp.max(scores, axis=-1, keepdims=True))
        weights = (expo / jnp.sum(expo, axis=-1, keepdims=True)).astype(BF16)
        context = lax.dot_general(
            weights, vbuf[rows], (((2,), (1,)), ((0,), (0,))), preferred_element_type=F32
        )
        ctx32[rows] = context

    for s in range(2):
        for g in range(4):
            ctxb[s * ROWS : (s + 1) * ROWS, g * HD : (g + 1) * HD] = ctx32[:, s * 4 + g, :].astype(BF16)

    def held(q, xx):
        return wbufs[q].at[xx % 2, :, c, :, xx // 2]

    def held_half(q, xx, half):
        return wbufs[q].at[xx % 2, pl.ds(half * 4, 4), c, :, xx // 2]

    def wait_a2a(q):
        some = sbufs[q].at[pl.ds(0, PLANE - 1)]
        remote(some, some, send_sem.at[q], a2a_sem.at[q], to_across).wait_recv()

    to_right = place(right, y, z, c)
    to_left = place(left, y, z, c)
    to_twin = place(x, y, z, 1 - c)

    def stage_one(q):
        mine = held(q, x)
        for side, where in enumerate((to_right, to_left)):
            remote(mine, mine, send_sem.at[3 + q], x1_sem.at[2 * q + side], where).start()
        remote(mine, mine, send_sem.at[7 + q], core_sem.at[q], to_twin).start()

    def stage_two(q):
        from_left, from_right = held(q, left), held(q, right)
        remote(from_left, from_left, send_sem.at[3 + q], x1_sem.at[2 * q], to_right).wait_recv()
        half = held_half(q, left, 0)
        remote(half, half, send_sem.at[5 + q], x2_sem.at[2 * q], to_right).start()
        remote(from_right, from_right, send_sem.at[3 + q], x1_sem.at[2 * q + 1], to_left).wait_recv()
        half = held_half(q, right, 1)
        remote(half, half, send_sem.at[5 + q], x2_sem.at[2 * q + 1], to_left).start()
        for part in (from_left, from_right):
            remote(part, part, send_sem.at[7 + q], core_sem.at[q], to_twin).start()

    def stage_three(q):
        for side in range(2):
            half = held_half(q, across, side)
            remote(half, half, send_sem.at[5 + q], x2_sem.at[2 * q + side], to_right).wait_recv()
        part = held(q, across)
        remote(part, part, send_sem.at[7 + q], core_sem.at[q], to_twin).start()

    wait_a2a(0)
    stage_one(0)

    load_wo.wait()

    @pl.loop(0, 8)
    def _(j):
        cols = pl.ds(pl.multiple_of(j * 512, 512), 512)
        partial = jnp.dot(ctxb[...], wo[:, cols], preferred_element_type=F32).astype(BF16)
        pbuf[j, 0] = partial[:ROWS]
        pbuf[j, 1] = partial[ROWS:]

    @pl.loop(1, 8)
    def _(o):
        yy = (y + o // 2) % NY
        hh = (h + o) % 2
        remote(
            pbuf.at[pl.ds(2 * yy, 2), hh],
            rsbuf.at[tp],
            send_sem.at[9],
            rs_sem,
            place(hh * 2 + x_lo, yy, z, c),
        ).start()

    rsbuf[tp] = pbuf[pl.ds(2 * y, 2), h]
    wait_a2a(1)
    stage_one(1)
    stage_two(0)

    some = rsbuf.at[pl.ds(0, 7)]
    remote(some, some, send_sem.at[9], rs_sem, to_across).wait_recv()
    remote(res.at[0], rres.at[0], send_sem.at[2], res_sem, to_across).wait_recv()
    for k in range(2):
        total = rsbuf[0, k].astype(F32)
        for i in range(1, 8):
            total = total + rsbuf[i, k].astype(F32)
        ybuf[2 * y + k] = (rres[k].astype(F32) + total).astype(BF16)

    mine = ybuf.at[pl.ds(2 * y, 2)]
    for o in range(1, NY):
        remote(mine, mine, send_sem.at[10], y_sem, place(x, (y + o) % NY, z, c)).start()
    remote(ybuf.at[2 * y + other], mixb.at[h], send_sem.at[11], mix_sem, to_across).start()
    mixb[h] = ybuf[2 * y + h]
    some = ybuf.at[pl.ds(0, 6)]
    remote(some, some, send_sem.at[10], y_sem, to_across).wait_recv()
    load_gain.wait()
    square = jnp.zeros((ROWS, 1), F32)
    for j in range(8):
        value = ybuf[j].astype(F32)
        square = square + jnp.sum(value * value, axis=-1, keepdims=True)
    factor = lax.rsqrt(square * (1.0 / D) + epsilon_norm)
    for j in range(8):
        cols = slice(j * 512, (j + 1) * 512)
        abuf[z, :, cols] = (
            ybuf[j].astype(F32) * factor * gain[:, cols].astype(F32)
        ).astype(BF16)

    to_up = place(x, y, z_up, c)
    to_dn = place(x, y, z_dn, c)

    def ring(step, up_ref, dn_ref):
        remote(up_ref, up_ref, send_sem.at[12], zr_sem.at[2 * step], to_up).start()
        remote(dn_ref, dn_ref, send_sem.at[12], zr_sem.at[2 * step + 1], to_dn).start()

    def ring_wait(step, up_ref, dn_ref):
        remote(up_ref, up_ref, send_sem.at[12], zr_sem.at[2 * step], to_up).wait_recv()
        remote(dn_ref, dn_ref, send_sem.at[12], zr_sem.at[2 * step + 1], to_dn).wait_recv()

    def block(shift):
        return abuf.at[(z + NZ + shift) % NZ]

    ring(0, block(0), block(0))
    stage_two(1)
    ring_wait(0, block(-1), block(1))
    ring(1, block(-1), block(1))
    stage_three(0)
    ring_wait(1, block(-2), block(2))
    ring(2, block(-2), block(2))
    ring_wait(2, block(-3), block(3))
    low, high = pl.ds(0, 16), pl.ds(16, 16)
    ring(3, block(-3).at[low], block(3).at[high])
    stage_three(1)
    ring_wait(3, block(4).at[low], block(4).at[high])

    def core_wait(q):
        both = wbufs[q].at[:, :, 1 - c]
        remote(both, both, send_sem.at[7 + q], core_sem.at[q], to_twin).wait_recv()

    scale = 1.0 / math.sqrt(D)

    def product(q):
        acts = jnp.zeros((NZ * ROWS, WIDTHS[q]), F32)
        for k in range(4):
            left_side = abuf[:, :, k * 1024 : (k + 1) * 1024].reshape(NZ * ROWS, 1024)
            right_side = wbufs[q][k // 2, (k % 2) * 4 : (k % 2) * 4 + 4].reshape(1024, WIDTHS[q])
            acts = acts + jnp.dot(left_side, right_side, preferred_element_type=F32)
        return acts * scale

    def gated(gate, upper):
        value = gate / (1.0 + jnp.exp(-gate)) * upper
        return value.astype(BF16).reshape(NZ, ROWS, 128)

    core_wait(0)
    acts = product(0)
    hbuf[:, :, 0:128] = gated(acts[:, 0:128], acts[:, 128:256])
    hbuf[:, :, 128:256] = gated(acts[:, 256:384], acts[:, 384:512])
    core_wait(1)
    acts = product(1)
    hbuf[:, :, 256:384] = gated(acts[:, 0:128], acts[:, 128:256])
    hbuf[:, :, 384:512] = gated(acts[:, 256:384], pltpu.roll(acts[:, 256:384], 64, 1))

    owner = (z // 4) * 2 + x_lo

    @pl.loop(1, NZ)
    def _(o):
        zz = (z + o) % NZ
        remote(
            hbuf.at[zz], obuf.at[h, z % 4], send_sem.at[13], out_sem, place(owner, y, zz, c)
        ).start()

    stays = z // 4 == h

    @pl.when(stays)
    def _():
        pltpu.make_async_copy(hbuf.at[z], obuf.at[h, z % 4], out_sem).start()

    @pl.when(jnp.logical_not(stays))
    def _():
        remote(
            hbuf.at[z], obuf.at[h, z % 4], send_sem.at[13], out_sem, place(across, y, z, c)
        ).start()

    remote(mixb.at[0], mixb.at[0], send_sem.at[11], mix_sem, to_across).wait_recv()
    store_mix = pltpu.make_async_copy(mixb, mix_out, store_sem.at[2])
    store_mix.start()

    remote(obuf, obuf, send_sem.at[13], out_sem, to_across).wait_recv()
    lane = lax.broadcasted_iota(jnp.int32, (2, ROWS, 128), 2)
    for p in range(2):
        even, odd = obuf[:, 2 * p], obuf[:, 2 * p + 1]
        base = p * PAIR
        hfin[:, :, base : base + 384] = even[:, :, 0:384]
        hfin[:, :, base + 384 : base + 512] = jnp.where(
            lane < 64, even[:, :, 384:512], odd[:, :, 384:512]
        )
        hfin[:, :, base + 512 : base + 896] = odd[:, :, 0:384]
    store_hid = pltpu.make_async_copy(hfin, hid_out, store_sem.at[3])
    store_hid.start()

    def sent(index, ref):
        remote(ref, ref, send_sem.at[index], mix_sem, to_across).wait_send()

    for q in range(2):
        sent(q, sbufs[q].at[pl.ds(0, PLANE - 1)])
        for _ in range(2):
            sent(3 + q, held(q, x))
        for _ in range(2):
            sent(5 + q, held_half(q, left, 0))
        sent(7 + q, wbufs[q].at[:, :, c])
    sent(2, res.at[0])
    sent(9, rsbuf.at[pl.ds(0, 7)])
    sent(10, ybuf.at[pl.ds(0, 6)])
    sent(11, ybuf.at[0])
    sent(12, abuf.at[pl.ds(0, 7)])
    sent(13, hbuf.at[pl.ds(0, 7)])

    @pl.when(jnp.logical_not(stays))
    def _():
        sent(13, hbuf.at[0])

    store_g.wait()
    store_u.wait()
    store_mix.wait()
    store_hid.wait()


def on_device(
    gate_param,
    up_param,
    gate_grad,
    up_grad,
    gate_mom,
    up_mom,
    gate_var,
    up_var,
    queries,
    new_keys,
    new_values,
    cache_keys,
    cache_values,
    cache_len,
    residual,
    out_proj,
    norm_gain,
):
    q_rows = queries.reshape(ROWS, 8, HD)
    pad = ((0, 0), (0, 14), (0, 0))
    keys_fresh = jnp.pad(new_keys, pad)
    vals_fresh = jnp.pad(new_values, pad)
    lens = jnp.broadcast_to(cache_len[:, None, None], (ROWS, 1, 128))
    res = residual.transpose(1, 0, 2)
    gain = norm_gain.reshape(1, D)
    dma = pltpu.SemaphoreType.DMA
    vmem = pltpu.VMEM
    anywhere = pl.BlockSpec(memory_space=pl.ANY)
    gate_updated, up_updated, mixed, hidden = pl.pallas_call(
        kernel,
        out_shape=(
            jax.ShapeDtypeStruct((16, FF), BF16),
            jax.ShapeDtypeStruct((16, FF), BF16),
            jax.ShapeDtypeStruct((2, ROWS, 512), BF16),
            jax.ShapeDtypeStruct((2, ROWS, 1792), BF16),
        ),
        in_specs=[anywhere] * 17,
        out_specs=[anywhere] * 4,
        scratch_shapes=[
            vmem((8, 16, FF), BF16),
            vmem((16, FF), BF16),
            vmem((16, FF), BF16),
            vmem((PLANE, 16, WIDTHS[0]), BF16),
            vmem((PLANE, 16, WIDTHS[1]), BF16),
            vmem((2, NZ, 2, NY, 2, 16, WIDTHS[0]), BF16),
            vmem((2, NZ, 2, NY, 2, 16, WIDTHS[1]), BF16),
            vmem((ROWS, 8, HD), BF16),
            vmem((ROWS, PADDED, HD), BF16),
            vmem((ROWS, PADDED, HD), BF16),
            vmem((ROWS, 1, 128), jnp.int32),
            vmem((2, ROWS, 512), BF16),
            vmem((512, D), BF16),
            vmem((1, D), BF16),
            vmem((ROWS, 8, HD), F32),
            vmem((2 * ROWS, 512), BF16),
            vmem((8, 2, ROWS, 512), BF16),
            vmem((8, 2, ROWS, 512), BF16),
            vmem((2, ROWS, 512), BF16),
            vmem((8, ROWS, 512), BF16),
            vmem((2, ROWS, 512), BF16),
            vmem((NZ, ROWS, D), BF16),
            vmem((NZ, ROWS, 512), BF16),
            vmem((2, 4, ROWS, 512), BF16),
            vmem((2, ROWS, 1792), BF16),
            dma((17,)),
            dma((14,)),
            dma((2,)),
            dma((4,)),
            dma((4,)),
            dma((2,)),
            dma(()),
            dma(()),
            dma(()),
            dma((8,)),
            dma(()),
            dma(()),
            dma((4,)),
        ],
        compiler_params=pltpu.CompilerParams(
            collective_id=0, has_side_effects=True, vmem_limit_bytes=56 * 1024 * 1024
        ),
    )(
        gate_param, up_param, gate_grad, up_grad, gate_mom, up_mom, gate_var, up_var,
        q_rows, keys_fresh, vals_fresh, cache_keys, cache_values, lens, res, out_proj, gain,
    )
    return (
        gate_updated,
        up_updated,
        mixed.transpose(1, 0, 2),
        hidden.transpose(1, 0, 2),
    )


def solution(mesh):
    both = P(("dp", "tp"), None)
    group = P("dp", None, "tp")
    return jax.shard_map(
        on_device,
        mesh=mesh,
        in_specs=(both,) * 8 + (group,) * 5 + (P("dp"), group, P("tp", None), P()),
        out_specs=(both, both, group, group),
        check_vma=False,
    )
```

```python
import functools
import math

import jax
import jax.numpy as jnp
from jax import lax
from jax.experimental import pallas as pl
from jax.experimental.pallas import tpu as pltpu
from jax.sharding import PartitionSpec as P

MESH = pl.DeviceIdType.MESH
F32 = jnp.float32
BF16 = jnp.bfloat16

HD = 128
ROWS = 32
SLOTS = 192
PADDED = 208
D = 4096
FF = 14336
NZ, NY = 8, 4
PLANE = NZ * NY
WIDTHS = (256, 256, 384)
CHUNKS = len(WIDTHS)
A2A, X1, X2, CORE, OUT = 0, 3, 6, 9, 12
RES, RS, GATHER, MIX, RING_A, RING_B, SPREAD = range(14, 21)
PAIR = 896

beta_one = 0.9
beta_two = 0.95
adam_step = 20
learn_rate = 0.1
decay_rate = 0.1
epsilon_adam = 1e-08
epsilon_norm = 1e-05
masked_score = -1e30


def adamw_update(param, grad, moment, second):
    grad32 = grad.astype(F32)
    moment_new = beta_one * moment.astype(F32) + (1.0 - beta_one) * grad32
    second_new = beta_two * second.astype(F32) + (1.0 - beta_two) * grad32 * grad32
    corr_one = 1.0 - beta_one**adam_step
    corr_two = 1.0 - beta_two**adam_step
    direction = moment_new * (1.0 / corr_one) / (
        jnp.sqrt(second_new * (1.0 / corr_two)) + epsilon_adam
    )
    param32 = param.astype(F32)
    return param32 - learn_rate * (direction + decay_rate * param32)


def kernel(
    len_in,
    gp, up, gg, ug, gm, um, gv, uv,
    q_in, nk_in, nv_in, ck_in, cv_in, res_in, wo_in, gain_in,
    g_out, u_out, mix_out, hid_out,
    adam, gnew, unew, sbuf0, sbuf1, sbuf2, wbuf0, wbuf1, wbuf2,
    raw, new_raw, raw32, new32, q32, res, kbuf, vbuf, wo, gain,
    ctx32, ctxb, pbuf, rsbuf, rres, ybuf, squares, abuf, bbuf, hbuf, gains,
    load_sem, send_sem, a2a_sem, x1_sem, x2_sem, core_sem,
    rs_sem, res_sem, y_sem, square_sem, za_sem, zb_sem, spread_sem, mix_sem, out_sem, store_sem,
):
    dp = lax.axis_index("dp")
    tp = lax.axis_index("tp")
    x_lo = dp // 16
    z = (dp // 2) % NZ
    c = dp % 2
    y = tp // 2
    h = tp % 2
    x = h * 2 + x_lo
    other = 1 - h

    def place(xx, yy, zz, cc):
        return ((xx % 2) * 16 + zz * 2 + cc, yy * 2 + xx // 2)

    right = (x + 1) % 4
    left = (x + 3) % 4
    across = (x + 2) % 4
    z_up = (z + 1) % NZ
    z_dn = (z + NZ - 1) % NZ

    load_q = pltpu.make_async_copy(q_in, raw.at[0], load_sem.at[8])
    load_res = pltpu.make_async_copy(res_in, raw.at[1], load_sem.at[9])
    load_nk = pltpu.make_async_copy(nk_in, new_raw.at[0], load_sem.at[10])
    load_nv = pltpu.make_async_copy(nv_in, new_raw.at[1], load_sem.at[11])
    load_k = pltpu.make_async_copy(ck_in, kbuf.at[:, pl.ds(0, SLOTS), :], load_sem.at[12])
    load_v = pltpu.make_async_copy(cv_in, vbuf.at[:, pl.ds(0, SLOTS), :], load_sem.at[13])
    load_wo = pltpu.make_async_copy(wo_in, wo, load_sem.at[14])
    load_gain = pltpu.make_async_copy(gain_in, gain, load_sem.at[15])
    for copy in (load_q, load_res, load_nk, load_nv):
        copy.start()
    loads = []
    for i, ref in enumerate((gp, gg, gm, gv, up, ug, um, uv)):
        loads.append(pltpu.make_async_copy(ref, adam.at[i], load_sem.at[i]))
    for copy in loads:
        copy.start()
    for copy in (load_k, load_v, load_wo, load_gain):
        copy.start()

    barrier = pltpu.get_barrier_semaphore()

    def greet(where):
        pl.semaphore_signal(barrier, inc=1, device_id=where, device_id_type=MESH)

    @pl.loop(1, PLANE)
    def _(o):
        greet(place(x, (y + o // NZ) % NY, (z + o % NZ) % NZ, c))

    @pl.loop(1, NZ)
    def _(o):
        greet(place(across, y, (z + o) % NZ, c))

    @pl.loop(0, NY)
    def _(o):
        greet(place(across, (y + o) % NY, z, c))

    greet(place(right, y, z, c))
    greet(place(left, y, z, c))
    greet(place(x, y, z, 1 - c))

    for copy in (load_q, load_res, load_nk, load_nv):
        copy.wait()
    for i in range(2):
        raw32[i] = raw[i].astype(F32)
    for s in range(2):
        for g in range(4):
            q32[:, s * 4 + g, :] = raw32[0, :, s, g * HD : (g + 1) * HD]
        res[s] = raw32[1, :, s, :].astype(BF16)
    for i, buf in enumerate((kbuf, vbuf)):
        new32[...] = jnp.zeros_like(new32)
        new32[:, 0:2, :] = new_raw[i].astype(F32)
        buf[:, SLOTS:PADDED, :] = new32[...].astype(BF16)

    sbufs = (sbuf0, sbuf1, sbuf2)
    wbufs = (wbuf0, wbuf1, wbuf2)

    def remote(src, dst, send, recv, where):
        return pltpu.make_async_remote_copy(
            src_ref=src,
            dst_ref=dst,
            send_sem=send,
            recv_sem=recv,
            device_id=where,
            device_id_type=MESH,
        )

    for copy in loads:
        copy.wait()
    pl.semaphore_wait(barrier, PLANE - 1 + NZ - 1 + NY + 3)
    position = y * NZ + z

    def updated(start, width):
        cols = pl.ds(pl.multiple_of(start, 128), width)
        tiles = []
        for first, dest in ((0, gnew), (4, unew)):
            value = adamw_update(
                adam[first, :, cols],
                adam[first + 1, :, cols],
                adam[first + 2, :, cols],
                adam[first + 3, :, cols],
            )
            dest[:, cols] = value.astype(BF16)
            tiles.append([value[:, i * 128 : (i + 1) * 128] for i in range(width // 128)])
        return tiles

    def fill(dest, tiles):
        for i, tile in enumerate(tiles):
            dest[:, i * 128 : (i + 1) * 128] = tile.astype(BF16)

    def send_block(q, dest):
        remote(
            sbufs[q].at[dest],
            wbufs[q].at[x_lo, z, c, y, h],
            send_sem.at[A2A + q],
            a2a_sem.at[q],
            place(x, dest // NZ, dest % NZ, c),
        ).start()

    def first_chunks(dest):
        gate, upper = updated((dest // 2) * PAIR + (dest % 2) * 512, 256)
        fill(sbuf0.at[dest], (gate[0], upper[0]))
        fill(sbuf1.at[dest], (gate[1], upper[1]))

    @pl.loop(1, PLANE)
    def _(t):
        dest = (position + t) % PLANE
        first_chunks(dest)
        send_block(0, dest)

    @pl.loop(1, PLANE)
    def _(t):
        send_block(1, (position + t) % PLANE)

    first_chunks(position)
    wbuf0[x_lo, z, c, y, h] = sbuf0[position]
    wbuf1[x_lo, z, c, y, h] = sbuf1[position]

    def last_chunk(pair):
        gate, upper = updated(pair * PAIR + 256, 256)
        last_gate, last_upper = updated(pair * PAIR + 768, 128)
        lane = lax.broadcasted_iota(jnp.int32, (16, 128), 1)
        turned = pltpu.roll(upper[1], 64, 1)
        even = jnp.where(lane < 64, gate[1], turned)
        odd = jnp.where(lane < 64, turned, gate[1])
        fill(sbuf2.at[2 * pair], (gate[0], upper[0], even))
        fill(sbuf2.at[2 * pair + 1], (last_gate[0], last_upper[0], odd))

    to_across = place(across, y, z, c)
    res_copy = remote(res.at[other], rres.at[h], send_sem.at[RES], res_sem, to_across)
    res_copy.start()
    rres[h] = res[h]

    load_k.wait()
    load_v.wait()
    part = 8

    @pl.loop(0, ROWS // part)
    def _(i):
        rows = pl.ds(pl.multiple_of(i * part, part), part)
        slot = lax.broadcasted_iota(jnp.int32, (part, 8, PADDED), 2)
        token = lax.broadcasted_iota(jnp.int32, (part, 8, PADDED), 1) // 4
        scores = lax.dot_general(
            q32[rows].astype(BF16), kbuf[rows], (((2,), (2,)), ((0,), (0,))), preferred_element_type=F32
        ) * (1.0 / math.sqrt(HD))
        filled = jnp.concatenate(
            [jnp.full((1, 8, PADDED), len_in[i * part + k], jnp.int32) for k in range(part)], axis=0
        )
        fresh = (slot >= SLOTS) & (slot <= SLOTS + token)
        scores = jnp.where((slot < filled) | fresh, scores, masked_score)
        expo = jnp.exp(scores - jnp.max(scores, axis=-1, keepdims=True))
        weights = (expo / jnp.sum(expo, axis=-1, keepdims=True)).astype(BF16)
        context = lax.dot_general(
            weights, vbuf[rows], (((2,), (1,)), ((0,), (0,))), preferred_element_type=F32
        )
        ctx32[rows] = context

    for s in range(2):
        for g in range(4):
            ctxb[s * ROWS : (s + 1) * ROWS, g * HD : (g + 1) * HD] = ctx32[:, s * 4 + g, :].astype(BF16)

    def held(q, xx):
        return wbufs[q].at[xx % 2, :, c, :, xx // 2]

    def held_half(q, xx, half):
        return wbufs[q].at[xx % 2, pl.ds(half * 4, 4), c, :, xx // 2]

    def wait_a2a(q):
        some = sbufs[q].at[pl.ds(0, PLANE - 1)]
        remote(some, some, send_sem.at[A2A + q], a2a_sem.at[q], to_across).wait_recv()

    to_right = place(right, y, z, c)
    to_left = place(left, y, z, c)
    to_twin = place(x, y, z, 1 - c)

    def stage_one(q):
        mine = held(q, x)
        for side, where in enumerate((to_right, to_left)):
            remote(mine, mine, send_sem.at[X1 + q], x1_sem.at[2 * q + side], where).start()
        remote(mine, mine, send_sem.at[CORE + q], core_sem.at[q], to_twin).start()

    def stage_two(q):
        from_left, from_right = held(q, left), held(q, right)
        remote(from_left, from_left, send_sem.at[X1 + q], x1_sem.at[2 * q], to_right).wait_recv()
        half = held_half(q, left, 0)
        remote(half, half, send_sem.at[X2 + q], x2_sem.at[2 * q], to_right).start()
        remote(from_right, from_right, send_sem.at[X1 + q], x1_sem.at[2 * q + 1], to_left).wait_recv()
        half = held_half(q, right, 1)
        remote(half, half, send_sem.at[X2 + q], x2_sem.at[2 * q + 1], to_left).start()
        for part in (from_left, from_right):
            remote(part, part, send_sem.at[CORE + q], core_sem.at[q], to_twin).start()

    def stage_three(q):
        for side in range(2):
            half = held_half(q, across, side)
            remote(half, half, send_sem.at[X2 + q], x2_sem.at[2 * q + side], to_right).wait_recv()
        part = held(q, across)
        remote(part, part, send_sem.at[CORE + q], core_sem.at[q], to_twin).start()

    wait_a2a(0)
    stage_one(0)

    load_wo.wait()

    @pl.loop(0, 8)
    def _(j):
        cols = pl.ds(pl.multiple_of(j * 512, 512), 512)
        partial = jnp.dot(ctxb[...], wo[:, cols], preferred_element_type=F32).astype(BF16)
        pbuf[j, 0] = partial[:ROWS]
        pbuf[j, 1] = partial[ROWS:]

    @pl.loop(1, 8)
    def _(o):
        yy = (y + o // 2) % NY
        hh = (h + o) % 2
        remote(
            pbuf.at[pl.ds(2 * yy, 2), hh],
            rsbuf.at[tp],
            send_sem.at[RS],
            rs_sem,
            place(hh * 2 + x_lo, yy, z, c),
        ).start()

    rsbuf[tp] = pbuf[pl.ds(2 * y, 2), h]

    @pl.loop(1, 16)
    def _(t):
        pair = (position // 2 + t) % 16
        last_chunk(pair)
        send_block(2, 2 * pair)
        send_block(2, 2 * pair + 1)

    last_chunk(position // 2)
    send_block(2, position + 1 - 2 * (position % 2))
    wbuf2[x_lo, z, c, y, h] = sbuf2[position]
    store_g = pltpu.make_async_copy(gnew, g_out, store_sem.at[0])
    store_u = pltpu.make_async_copy(unew, u_out, store_sem.at[1])
    store_g.start()
    store_u.start()

    wait_a2a(1)
    stage_one(1)

    some = rsbuf.at[pl.ds(0, 7)]
    remote(some, some, send_sem.at[RS], rs_sem, to_across).wait_recv()
    remote(res.at[0], rres.at[0], send_sem.at[RES], res_sem, to_across).wait_recv()
    square = jnp.zeros((ROWS, 1), F32)
    for k in range(2):
        total = rsbuf[0, k].astype(F32)
        for i in range(1, 8):
            total = total + rsbuf[i, k].astype(F32)
        ybuf[2 * y + k] = (rres[k].astype(F32) + total).astype(BF16)
        value = ybuf[2 * y + k].astype(F32)
        square = square + jnp.sum(value * value, axis=-1, keepdims=True)
    squares[y] = jnp.broadcast_to(square, (ROWS, 128))

    y_peers = [place(x, (y + o) % NY, z, c) for o in range(1, NY)]
    for where in y_peers:
        remote(squares.at[y], squares.at[y], send_sem.at[GATHER], square_sem, where).start()
    for where in y_peers:
        mine = ybuf.at[2 * y]
        remote(mine, mine, send_sem.at[GATHER], y_sem, where).start()
    remote(ybuf.at[2 * y + other], mix_out.at[h], send_sem.at[MIX], mix_sem, to_across).start()
    store_mix = pltpu.make_async_copy(ybuf.at[2 * y + h], mix_out.at[h], store_sem.at[2])
    store_mix.start()
    load_gain.wait()
    gain32 = gain[...].astype(F32).reshape(1, D)
    for j in range(8):
        gains[j] = gain32[:, j * 512 : (j + 1) * 512]
    some = squares.at[pl.ds(0, 3)]
    remote(some, some, send_sem.at[GATHER], square_sem, to_across).wait_recv()
    square = (squares[0] + squares[1] + squares[2] + squares[3])[:, 0:1]
    factor = lax.rsqrt(square * (1.0 / D) + epsilon_norm)
    bbuf[z, y] = (ybuf[2 * y + 1].astype(F32) * factor * gains[2 * y + 1]).astype(BF16)

    to_up = place(x, y, z_up, c)
    to_dn = place(x, y, z_dn, c)

    def ring(kind, step, up_ref, dn_ref):
        sems = zb_sem if kind == RING_B else za_sem
        remote(up_ref, up_ref, send_sem.at[kind], sems.at[2 * step], to_up).start()
        remote(dn_ref, dn_ref, send_sem.at[kind], sems.at[2 * step + 1], to_dn).start()

    def ring_wait(kind, step, up_ref, dn_ref):
        sems = zb_sem if kind == RING_B else za_sem
        remote(up_ref, up_ref, send_sem.at[kind], sems.at[2 * step], to_up).wait_recv()
        remote(dn_ref, dn_ref, send_sem.at[kind], sems.at[2 * step + 1], to_dn).wait_recv()

    def block(shift):
        return abuf.at[(z + NZ + shift) % NZ]

    def block_b(shift):
        return bbuf.at[(z + NZ + shift) % NZ, y]

    def spread(shift):
        for where in y_peers:
            part = block_b(shift)
            remote(part, part, send_sem.at[SPREAD], spread_sem, where).start()

    low, high = pl.ds(0, 16), pl.ds(16, 16)
    ring(RING_B, 0, block_b(0), block_b(0))
    spread(0)
    some = ybuf.at[pl.ds(0, 3)]
    remote(some, some, send_sem.at[GATHER], y_sem, to_across).wait_recv()
    for k in range(4):
        abuf[z, :, k * 512 : (k + 1) * 512] = (
            ybuf[2 * k].astype(F32) * factor * gains[2 * k]
        ).astype(BF16)
    ring(RING_A, 0, block(0), block(0))
    ring_wait(RING_B, 0, block_b(-1), block_b(1))
    ring(RING_B, 1, block_b(-1), block_b(1))
    spread(-1)
    spread(1)
    stage_two(0)
    ring_wait(RING_B, 1, block_b(-2), block_b(2))
    ring(RING_B, 2, block_b(-2), block_b(2))
    spread(-2)
    spread(2)
    wait_a2a(2)
    stage_one(2)
    ring_wait(RING_A, 0, block(-1), block(1))
    ring(RING_A, 1, block(-1), block(1))
    ring_wait(RING_B, 2, block_b(-3), block_b(3))
    ring(RING_B, 3, block_b(-3).at[low], block_b(3).at[high])
    spread(-3)
    spread(3)
    stage_two(1)
    stage_three(0)
    ring_wait(RING_A, 1, block(-2), block(2))
    ring(RING_A, 2, block(-2), block(2))
    ring_wait(RING_B, 3, block_b(4).at[low], block_b(4).at[high])
    spread(4)
    stage_three(1)
    ring_wait(RING_A, 2, block(-3), block(3))
    ring(RING_A, 3, block(-3).at[low], block(3).at[high])
    stage_two(2)
    ring_wait(RING_A, 3, block(4).at[low], block(4).at[high])
    some = abuf.at[pl.ds(0, 6)]
    remote(some, some, send_sem.at[SPREAD], spread_sem, to_across).wait_recv()

    def core_wait(q):
        both = wbufs[q].at[:, :, 1 - c]
        remote(both, both, send_sem.at[CORE + q], core_sem.at[q], to_twin).wait_recv()

    scale = 1.0 / math.sqrt(D)

    def product(q):
        acts = jnp.zeros((NZ * ROWS, WIDTHS[q]), F32)
        for j in range(8):
            if j % 2 == 0:
                left_side = abuf[:, :, j * 256 : j * 256 + 512]
            else:
                left_side = bbuf[:, j // 2]
            first = (j % 4) * 2
            right_side = wbufs[q][j // 4, first : first + 2].reshape(512, WIDTHS[q])
            acts = acts + jnp.dot(
                left_side.reshape(NZ * ROWS, 512), right_side, preferred_element_type=F32
            )
        return acts * scale

    def gated(gate, upper):
        value = gate / (1.0 + jnp.exp(-gate)) * upper
        return value.astype(BF16).reshape(NZ, ROWS, 128)

    owner = (z // 4) * 2 + x_lo
    stays = z // 4 == h

    def send_hidden(q):
        @pl.loop(1, NZ)
        def _(o):
            zz = (z + o) % NZ
            remote(
                hbuf.at[q, zz],
                hid_out.at[q, h, z % 4],
                send_sem.at[OUT + q],
                out_sem.at[q],
                place(owner, y, zz, c),
            ).start()

        @pl.when(stays)
        def _():
            pltpu.make_async_copy(hbuf.at[q, z], hid_out.at[q, h, z % 4], out_sem.at[q]).start()

        @pl.when(jnp.logical_not(stays))
        def _():
            remote(
                hbuf.at[q, z],
                hid_out.at[q, h, z % 4],
                send_sem.at[OUT + q],
                out_sem.at[q],
                to_across,
            ).start()

    core_wait(0)
    acts = product(0)
    hbuf[0, :, :, 0:128] = gated(acts[:, 0:128], acts[:, 128:256])
    core_wait(1)
    acts = product(1)
    hbuf[0, :, :, 128:256] = gated(acts[:, 0:128], acts[:, 128:256])
    send_hidden(0)
    stage_three(2)
    core_wait(2)
    acts = product(2)
    hbuf[1, :, :, 0:128] = gated(acts[:, 0:128], acts[:, 128:256])
    hbuf[1, :, :, 128:256] = gated(acts[:, 256:384], pltpu.roll(acts[:, 256:384], 64, 1))
    send_hidden(1)

    remote(mix_out.at[0], mix_out.at[0], send_sem.at[MIX], mix_sem, to_across).wait_recv()
    for q in range(2):
        whole = hid_out.at[q]
        remote(whole, whole, send_sem.at[OUT + q], out_sem.at[q], to_across).wait_recv()

    def sent(index, ref):
        remote(ref, ref, send_sem.at[index], mix_sem, to_across).wait_send()

    for q in range(CHUNKS):
        sent(A2A + q, sbufs[q].at[pl.ds(0, PLANE - 1)])
        for _ in range(2):
            sent(X1 + q, held(q, x))
        for _ in range(2):
            sent(X2 + q, held_half(q, left, 0))
        sent(CORE + q, wbufs[q].at[:, :, c])
    sent(RES, res.at[0])
    sent(RS, rsbuf.at[pl.ds(0, 7)])
    sent(GATHER, squares.at[pl.ds(0, 3)])
    sent(GATHER, ybuf.at[pl.ds(0, 3)])
    sent(MIX, ybuf.at[0])
    sent(RING_A, abuf.at[pl.ds(0, 7)])
    sent(RING_B, bbuf.at[pl.ds(0, 7), 0])
    sent(SPREAD, abuf.at[pl.ds(0, 6)])
    for q in range(2):
        sent(OUT + q, hbuf.at[q, pl.ds(0, 7)])

    @pl.when(jnp.logical_not(stays))
    def _():
        for q in range(2):
            sent(OUT + q, hbuf.at[q, 0])

    store_g.wait()
    store_u.wait()
    store_mix.wait()


def finish(
    g_in, u_in, mix_in, hid_in, g_out, u_out, mix_out, hid_out, shards, mix32, hid32, sem
):
    halves = [pl.ds(0, FF // 2), pl.ds(FF // 2, FF // 2)]
    load, store = [], []
    for i, (source, dest) in enumerate(((g_in, g_out), (u_in, u_out))):
        for k, cols in enumerate(halves):
            held = shards.at[i, :, cols]
            load.append(pltpu.make_async_copy(source.at[:, cols], held, sem.at[2 * i + k]))
            store.append(pltpu.make_async_copy(held, dest.at[:, cols], sem.at[4 + 2 * i + k]))
    for copy in load:
        copy.start()
    lane = lax.broadcasted_iota(jnp.int32, (ROWS, 128), 1)
    for s in range(2):
        mix32[:, s, :] = mix_in[s].astype(F32)
        for p in range(2):
            even, odd = 2 * p, 2 * p + 1
            base = p * PAIR
            middle = jnp.where(
                lane < 64,
                hid_in[1, s, even, :, 128:256].astype(F32),
                hid_in[1, s, odd, :, 128:256].astype(F32),
            )
            hid32[:, s, base : base + 256] = hid_in[0, s, even].astype(F32)
            hid32[:, s, base + 256 : base + 384] = hid_in[1, s, even, :, 0:128].astype(F32)
            hid32[:, s, base + 384 : base + 512] = middle
            hid32[:, s, base + 512 : base + 768] = hid_in[0, s, odd].astype(F32)
            hid32[:, s, base + 768 : base + 896] = hid_in[1, s, odd, :, 0:128].astype(F32)
    for first, second in zip(load, store):
        first.wait()
        second.start()
    mix_out[...] = mix32[...].astype(BF16)
    hid_out[...] = hid32[...].astype(BF16)
    for copy in store:
        copy.wait()


def on_device(
    gate_param,
    up_param,
    gate_grad,
    up_grad,
    gate_mom,
    up_mom,
    gate_var,
    up_var,
    queries,
    new_keys,
    new_values,
    cache_keys,
    cache_values,
    cache_len,
    residual,
    out_proj,
    norm_gain,
):
    dma = pltpu.SemaphoreType.DMA
    vmem = pltpu.VMEM
    anywhere = pl.BlockSpec(memory_space=pl.ANY)
    inside = pl.BlockSpec(memory_space=vmem)
    shard = jax.ShapeDtypeStruct((16, FF), BF16)
    gate_updated, up_updated, mixed, hidden = pl.pallas_call(
        kernel,
        out_shape=(
            shard,
            shard,
            jax.ShapeDtypeStruct((2, ROWS, 512), BF16),
            jax.ShapeDtypeStruct((2, 2, 4, ROWS, 256), BF16),
        ),
        in_specs=[pl.BlockSpec(memory_space=pltpu.SMEM)] + [anywhere] * 16,
        out_specs=[anywhere] * 4,
        scratch_shapes=[
            vmem((8, 16, FF), BF16),
            vmem((16, FF), BF16),
            vmem((16, FF), BF16),
            *[vmem((PLANE, 16, width), BF16) for width in WIDTHS],
            *[vmem((2, NZ, 2, NY, 2, 16, width), BF16) for width in WIDTHS],
            vmem((2, ROWS, 2, 512), BF16),
            vmem((2, ROWS, 2, HD), BF16),
            vmem((2, ROWS, 2, 512), F32),
            vmem((ROWS, 16, HD), F32),
            vmem((ROWS, 8, HD), F32),
            vmem((2, ROWS, 512), BF16),
            vmem((ROWS, PADDED, HD), BF16),
            vmem((ROWS, PADDED, HD), BF16),
            vmem((512, D), BF16),
            vmem((D,), BF16),
            vmem((ROWS, 8, HD), F32),
            vmem((2 * ROWS, 512), BF16),
            vmem((8, 2, ROWS, 512), BF16),
            vmem((8, 2, ROWS, 512), BF16),
            vmem((2, ROWS, 512), BF16),
            vmem((8, ROWS, 512), BF16),
            vmem((NY, ROWS, 128), F32),
            vmem((NZ, ROWS, D // 2), BF16),
            vmem((NZ, NY, ROWS, 512), BF16),
            vmem((2, NZ, ROWS, 256), BF16),
            vmem((8, 1, 512), F32),
            dma((16,)),
            dma((21,)),
            dma((CHUNKS,)),
            dma((2 * CHUNKS,)),
            dma((2 * CHUNKS,)),
            dma((CHUNKS,)),
            dma(()),
            dma(()),
            dma(()),
            dma(()),
            dma((8,)),
            dma((8,)),
            dma(()),
            dma(()),
            dma((2,)),
            dma((3,)),
        ],
        compiler_params=pltpu.CompilerParams(
            collective_id=0, has_side_effects=True, vmem_limit_bytes=56 * 1024 * 1024
        ),
    )(
        cache_len,
        gate_param, up_param, gate_grad, up_grad, gate_mom, up_mom, gate_var, up_var,
        queries, new_keys, new_values, cache_keys, cache_values, residual, out_proj, norm_gain,
    )
    return pl.pallas_call(
        finish,
        out_shape=(
            shard,
            shard,
            jax.ShapeDtypeStruct((ROWS, 2, 512), BF16),
            jax.ShapeDtypeStruct((ROWS, 2, 1792), BF16),
        ),
        in_specs=[anywhere, anywhere, inside, inside],
        out_specs=(anywhere, anywhere, inside, inside),
        scratch_shapes=[
            vmem((2, 16, FF), BF16),
            vmem((ROWS, 2, 512), F32),
            vmem((ROWS, 2, 1792), F32),
            dma((8,)),
        ],
        compiler_params=pltpu.CompilerParams(vmem_limit_bytes=56 * 1024 * 1024),
    )(gate_updated, up_updated, mixed, hidden)


def solution(mesh):
    both = P(("dp", "tp"), None)
    group = P("dp", None, "tp")
    return jax.shard_map(
        on_device,
        mesh=mesh,
        in_specs=(both,) * 8 + (group,) * 5 + (P("dp"), group, P("tp", None), P()),
        out_specs=(both, both, group, group),
        check_vma=False,
    )
```

```python
import functools
import math

import jax
import jax.numpy as jnp
from jax import lax
from jax.experimental import pallas as pl
from jax.experimental.pallas import tpu as pltpu
from jax.sharding import PartitionSpec as P

MESH = pl.DeviceIdType.MESH
F32 = jnp.float32
BF16 = jnp.bfloat16

HD = 128
ROWS = 32
SLOTS = 192
PADDED = 208
D = 4096
FF = 14336
NZ, NY = 8, 4
PLANE = NZ * NY
WIDTHS = (256, 256, 384)
CHUNKS = len(WIDTHS)
A2A, X1, X2, CORE, OUT = 0, 3, 6, 9, 12
RES, RS, GATHER, MIX, SPREAD, RING = range(14, 20)
PAIR = 896

beta_one = 0.9
beta_two = 0.95
adam_step = 20
learn_rate = 0.1
decay_rate = 0.1
epsilon_adam = 1e-08
epsilon_norm = 1e-05
masked_score = -1e30


def adamw_update(param, grad, moment, second):
    grad32 = grad.astype(F32)
    moment_new = beta_one * moment.astype(F32) + (1.0 - beta_one) * grad32
    second_new = beta_two * second.astype(F32) + (1.0 - beta_two) * grad32 * grad32
    corr_one = 1.0 - beta_one**adam_step
    corr_two = 1.0 - beta_two**adam_step
    direction = moment_new * (1.0 / corr_one) / (
        jnp.sqrt(second_new * (1.0 / corr_two)) + epsilon_adam
    )
    param32 = param.astype(F32)
    return param32 - learn_rate * (direction + decay_rate * param32)


def kernel(
    len_in,
    gp, up, gg, ug, gm, um, gv, uv,
    q_in, nk_in, nv_in, ck_in, cv_in, res_in, wo_in, gain_in,
    g_out, u_out, mix_out, hid_out,
    adam, gnew, unew, sbuf0, sbuf1, sbuf2, wbuf0, wbuf1, wbuf2,
    raw, new_raw, raw32, new32, q32, res, kbuf, vbuf, wo, gain,
    ctx32, ctxb, pbuf, rsbuf, rres, ybuf, squares, abuf, bbuf, hbuf, gains,
    load_sem, send_sem, a2a_sem, x1_sem, x2_sem, core_sem,
    rs_sem, res_sem, y_sem, square_sem, z_sem, spread_sem, mix_sem, out_sem, store_sem,
):
    dp = lax.axis_index("dp")
    tp = lax.axis_index("tp")
    x_lo = dp // 16
    z = (dp // 2) % NZ
    c = dp % 2
    y = tp // 2
    h = tp % 2
    x = h * 2 + x_lo
    other = 1 - h

    def place(xx, yy, zz, cc):
        return ((xx % 2) * 16 + zz * 2 + cc, yy * 2 + xx // 2)

    right = (x + 1) % 4
    left = (x + 3) % 4
    across = (x + 2) % 4
    z_up = (z + 1) % NZ
    z_dn = (z + NZ - 1) % NZ

    load_q = pltpu.make_async_copy(q_in, raw.at[0], load_sem.at[8])
    load_res = pltpu.make_async_copy(res_in, raw.at[1], load_sem.at[9])
    load_nk = pltpu.make_async_copy(nk_in, new_raw.at[0], load_sem.at[10])
    load_nv = pltpu.make_async_copy(nv_in, new_raw.at[1], load_sem.at[11])
    load_k = pltpu.make_async_copy(ck_in, kbuf.at[:, pl.ds(0, SLOTS), :], load_sem.at[12])
    load_v = pltpu.make_async_copy(cv_in, vbuf.at[:, pl.ds(0, SLOTS), :], load_sem.at[13])
    load_wo = pltpu.make_async_copy(wo_in, wo, load_sem.at[14])
    load_gain = pltpu.make_async_copy(gain_in, gain, load_sem.at[15])
    for copy in (load_q, load_res, load_nk, load_nv):
        copy.start()
    loads = []
    for i, ref in enumerate((gp, gg, gm, gv, up, ug, um, uv)):
        loads.append(pltpu.make_async_copy(ref, adam.at[i], load_sem.at[i]))
    for copy in loads:
        copy.start()
    for copy in (load_k, load_v, load_wo, load_gain):
        copy.start()

    barrier = pltpu.get_barrier_semaphore()

    def greet(where):
        pl.semaphore_signal(barrier, inc=1, device_id=where, device_id_type=MESH)

    @pl.loop(1, PLANE)
    def _(o):
        greet(place(x, (y + o // NZ) % NY, (z + o % NZ) % NZ, c))

    @pl.loop(1, NZ)
    def _(o):
        greet(place(across, y, (z + o) % NZ, c))

    @pl.loop(0, NY)
    def _(o):
        greet(place(across, (y + o) % NY, z, c))

    greet(place(right, y, z, c))
    greet(place(left, y, z, c))
    greet(place(x, y, z, 1 - c))

    for copy in (load_q, load_res, load_nk, load_nv):
        copy.wait()
    for i in range(2):
        raw32[i] = raw[i].astype(F32)
    for s in range(2):
        for g in range(4):
            q32[:, s * 4 + g, :] = raw32[0, :, s, g * HD : (g + 1) * HD]
        res[s] = raw32[1, :, s, :].astype(BF16)
    for i, buf in enumerate((kbuf, vbuf)):
        new32[...] = jnp.zeros_like(new32)
        new32[:, 0:2, :] = new_raw[i].astype(F32)
        buf[:, SLOTS:PADDED, :] = new32[...].astype(BF16)

    sbufs = (sbuf0, sbuf1, sbuf2)
    wbufs = (wbuf0, wbuf1, wbuf2)

    def remote(src, dst, send, recv, where):
        return pltpu.make_async_remote_copy(
            src_ref=src,
            dst_ref=dst,
            send_sem=send,
            recv_sem=recv,
            device_id=where,
            device_id_type=MESH,
        )

    for copy in loads:
        copy.wait()
    pl.semaphore_wait(barrier, PLANE - 1 + NZ - 1 + NY + 3)
    position = y * NZ + z

    def updated(start, width):
        cols = pl.ds(pl.multiple_of(start, 128), width)
        tiles = []
        for first, dest in ((0, gnew), (4, unew)):
            value = adamw_update(
                adam[first, :, cols],
                adam[first + 1, :, cols],
                adam[first + 2, :, cols],
                adam[first + 3, :, cols],
            )
            dest[:, cols] = value.astype(BF16)
            tiles.append([value[:, i * 128 : (i + 1) * 128] for i in range(width // 128)])
        return tiles

    def fill(dest, tiles):
        for i, tile in enumerate(tiles):
            dest[:, i * 128 : (i + 1) * 128] = tile.astype(BF16)

    def send_block(q, dest):
        remote(
            sbufs[q].at[dest],
            wbufs[q].at[x_lo, z, c, y, h],
            send_sem.at[A2A + q],
            a2a_sem.at[q],
            place(x, dest // NZ, dest % NZ, c),
        ).start()

    def first_chunks(dest):
        gate, upper = updated((dest // 2) * PAIR + (dest % 2) * 512, 256)
        fill(sbuf0.at[dest], (gate[0], upper[0]))
        fill(sbuf1.at[dest], (gate[1], upper[1]))

    @pl.loop(1, PLANE)
    def _(t):
        dest = (position + t) % PLANE
        first_chunks(dest)
        send_block(0, dest)

    @pl.loop(1, PLANE)
    def _(t):
        send_block(1, (position + t) % PLANE)

    first_chunks(position)
    wbuf0[x_lo, z, c, y, h] = sbuf0[position]
    wbuf1[x_lo, z, c, y, h] = sbuf1[position]

    def last_chunk(pair):
        gate, upper = updated(pair * PAIR + 256, 256)
        last_gate, last_upper = updated(pair * PAIR + 768, 128)
        lane = lax.broadcasted_iota(jnp.int32, (16, 128), 1)
        turned = pltpu.roll(upper[1], 64, 1)
        even = jnp.where(lane < 64, gate[1], turned)
        odd = jnp.where(lane < 64, turned, gate[1])
        fill(sbuf2.at[2 * pair], (gate[0], upper[0], even))
        fill(sbuf2.at[2 * pair + 1], (last_gate[0], last_upper[0], odd))

    to_across = place(across, y, z, c)
    res_copy = remote(res.at[other], rres.at[h], send_sem.at[RES], res_sem, to_across)
    res_copy.start()
    rres[h] = res[h]

    load_k.wait()
    load_v.wait()
    part = 8

    @pl.loop(0, ROWS // part)
    def _(i):
        rows = pl.ds(pl.multiple_of(i * part, part), part)
        slot = lax.broadcasted_iota(jnp.int32, (part, 8, PADDED), 2)
        token = lax.broadcasted_iota(jnp.int32, (part, 8, PADDED), 1) // 4
        scores = lax.dot_general(
            q32[rows].astype(BF16), kbuf[rows], (((2,), (2,)), ((0,), (0,))), preferred_element_type=F32
        ) * (1.0 / math.sqrt(HD))
        filled = jnp.concatenate(
            [jnp.full((1, 8, PADDED), len_in[i * part + k], jnp.int32) for k in range(part)], axis=0
        )
        fresh = (slot >= SLOTS) & (slot <= SLOTS + token)
        scores = jnp.where((slot < filled) | fresh, scores, masked_score)
        expo = jnp.exp(scores - jnp.max(scores, axis=-1, keepdims=True))
        weights = (expo / jnp.sum(expo, axis=-1, keepdims=True)).astype(BF16)
        context = lax.dot_general(
            weights, vbuf[rows], (((2,), (1,)), ((0,), (0,))), preferred_element_type=F32
        )
        ctx32[rows] = context

    for s in range(2):
        for g in range(4):
            ctxb[s * ROWS : (s + 1) * ROWS, g * HD : (g + 1) * HD] = ctx32[:, s * 4 + g, :].astype(BF16)

    def held(q, xx):
        return wbufs[q].at[xx % 2, :, c, :, xx // 2]

    def held_half(q, xx, half):
        return wbufs[q].at[xx % 2, pl.ds(half * 4, 4), c, :, xx // 2]

    def wait_a2a(q):
        some = sbufs[q].at[pl.ds(0, PLANE - 1)]
        remote(some, some, send_sem.at[A2A + q], a2a_sem.at[q], to_across).wait_recv()

    to_right = place(right, y, z, c)
    to_left = place(left, y, z, c)
    to_twin = place(x, y, z, 1 - c)

    def stage_one(q):
        mine = held(q, x)
        for side, where in enumerate((to_right, to_left)):
            remote(mine, mine, send_sem.at[X1 + q], x1_sem.at[2 * q + side], where).start()
        remote(mine, mine, send_sem.at[CORE + q], core_sem.at[q], to_twin).start()

    def stage_two(q):
        from_left, from_right = held(q, left), held(q, right)
        remote(from_left, from_left, send_sem.at[X1 + q], x1_sem.at[2 * q], to_right).wait_recv()
        half = held_half(q, left, 0)
        remote(half, half, send_sem.at[X2 + q], x2_sem.at[2 * q], to_right).start()
        remote(from_right, from_right, send_sem.at[X1 + q], x1_sem.at[2 * q + 1], to_left).wait_recv()
        half = held_half(q, right, 1)
        remote(half, half, send_sem.at[X2 + q], x2_sem.at[2 * q + 1], to_left).start()
        for part in (from_left, from_right):
            remote(part, part, send_sem.at[CORE + q], core_sem.at[q], to_twin).start()

    def stage_three(q):
        for side in range(2):
            half = held_half(q, across, side)
            remote(half, half, send_sem.at[X2 + q], x2_sem.at[2 * q + side], to_right).wait_recv()
        part = held(q, across)
        remote(part, part, send_sem.at[CORE + q], core_sem.at[q], to_twin).start()

    load_wo.wait()

    @pl.loop(0, 8)
    def _(j):
        cols = pl.ds(pl.multiple_of(j * 512, 512), 512)
        partial = jnp.dot(ctxb[...], wo[:, cols], preferred_element_type=F32).astype(BF16)
        pbuf[j, 0] = partial[:ROWS]
        pbuf[j, 1] = partial[ROWS:]

    @pl.loop(1, 8)
    def _(o):
        yy = (y + o // 2) % NY
        hh = (h + o) % 2
        remote(
            pbuf.at[pl.ds(2 * yy, 2), hh],
            rsbuf.at[tp],
            send_sem.at[RS],
            rs_sem,
            place(hh * 2 + x_lo, yy, z, c),
        ).start()

    rsbuf[tp] = pbuf[pl.ds(2 * y, 2), h]

    @pl.loop(1, 16)
    def _(t):
        pair = (position // 2 + t) % 16
        last_chunk(pair)
        send_block(2, 2 * pair)
        send_block(2, 2 * pair + 1)

    last_chunk(position // 2)
    send_block(2, position + 1 - 2 * (position % 2))
    wbuf2[x_lo, z, c, y, h] = sbuf2[position]
    store_g = pltpu.make_async_copy(gnew, g_out, store_sem.at[0])
    store_u = pltpu.make_async_copy(unew, u_out, store_sem.at[1])
    store_g.start()
    store_u.start()

    wait_a2a(0)
    stage_one(0)

    some = rsbuf.at[pl.ds(0, 7)]
    remote(some, some, send_sem.at[RS], rs_sem, to_across).wait_recv()
    remote(res.at[0], rres.at[0], send_sem.at[RES], res_sem, to_across).wait_recv()
    square = jnp.zeros((ROWS, 1), F32)
    for k in range(2):
        total = rsbuf[0, k].astype(F32)
        for i in range(1, 8):
            total = total + rsbuf[i, k].astype(F32)
        ybuf[2 * y + k] = (rres[k].astype(F32) + total).astype(BF16)
        value = ybuf[2 * y + k].astype(F32)
        square = square + jnp.sum(value * value, axis=-1, keepdims=True)
    squares[y] = jnp.broadcast_to(square, (ROWS, 128))

    y_peers = [place(x, (y + o) % NY, z, c) for o in range(1, NY)]
    for where in y_peers:
        remote(squares.at[y], squares.at[y], send_sem.at[GATHER], square_sem, where).start()
    for where in y_peers:
        mine = ybuf.at[2 * y]
        remote(mine, mine, send_sem.at[GATHER], y_sem, where).start()
    remote(ybuf.at[2 * y + other], mix_out.at[h], send_sem.at[MIX], mix_sem, to_across).start()
    store_mix = pltpu.make_async_copy(ybuf.at[2 * y + h], mix_out.at[h], store_sem.at[2])
    store_mix.start()
    wait_a2a(1)
    stage_one(1)
    load_gain.wait()
    gain32 = gain[...].astype(F32).reshape(1, D)
    for j in range(8):
        gains[j] = gain32[:, j * 512 : (j + 1) * 512]
    some = squares.at[pl.ds(0, 3)]
    remote(some, some, send_sem.at[GATHER], square_sem, to_across).wait_recv()
    square = (squares[0] + squares[1] + squares[2] + squares[3])[:, 0:1]
    factor = lax.rsqrt(square * (1.0 / D) + epsilon_norm)
    bbuf[z, y] = (ybuf[2 * y + 1].astype(F32) * factor * gains[2 * y + 1]).astype(BF16)

    to_up = place(x, y, z_up, c)
    to_dn = place(x, y, z_dn, c)

    def block(chain, shift):
        zz = (z + NZ + shift) % NZ
        return bbuf.at[zz, y] if chain == 2 else abuf.at[chain, zz]

    to_side = (to_up, to_dn)

    def ring_copy(chain, step, side, part):
        return remote(
            part, part, send_sem.at[RING + chain], z_sem.at[chain * 8 + step * 2 + side], to_side[side]
        )

    def ring_part(chain, step, side):
        part = block(chain, (-step, step)[side])
        return part.at[pl.ds(side * 16, 16)] if step == 3 else part

    def ring_send(chain, step, side):
        ring_copy(chain, step, side, ring_part(chain, step, side)).start()

    def ring_take(chain, step, side):
        shift = (-step - 1, step + 1)[side]
        part = block(chain, shift)
        if step == 3:
            part = part.at[pl.ds(side * 16, 16)]
        ring_copy(chain, step, side, part).wait_recv()

    def spread(shift):
        for where in y_peers:
            part = block(2, shift)
            remote(part, part, send_sem.at[SPREAD], spread_sem, where).start()

    def advance(chain, step):
        for side in range(2):
            ring_take(chain, step, side)
            if step < 3:
                ring_send(chain, step + 1, side)
        if chain == 2:
            if step < 3:
                spread(-step - 1)
                spread(step + 1)
            else:
                spread(4)

    for side in range(2):
        ring_send(2, 0, side)
    spread(0)
    some = ybuf.at[pl.ds(0, 3)]
    remote(some, some, send_sem.at[GATHER], y_sem, to_across).wait_recv()
    for chain in range(2):
        for k in range(2):
            j = 4 * chain + 2 * k
            abuf[chain, z, :, k * 512 : (k + 1) * 512] = (
                ybuf[j].astype(F32) * factor * gains[j]
            ).astype(BF16)
        for side in range(2):
            ring_send(chain, 0, side)
    stage_two(0)
    advance(2, 0)
    advance(0, 0)
    advance(1, 0)
    advance(2, 1)
    wait_a2a(2)
    stage_one(2)
    advance(0, 1)
    advance(1, 1)
    advance(2, 2)
    stage_two(1)
    advance(0, 2)
    advance(1, 2)
    advance(2, 3)
    stage_three(0)
    advance(0, 3)
    advance(1, 3)
    stage_two(2)
    stage_three(1)
    some = abuf.at[:, pl.ds(0, 6)]
    remote(some, some, send_sem.at[SPREAD], spread_sem, to_across).wait_recv()

    def core_wait(q):
        both = wbufs[q].at[:, :, 1 - c]
        remote(both, both, send_sem.at[CORE + q], core_sem.at[q], to_twin).wait_recv()

    scale = 1.0 / math.sqrt(D)

    def product(q):
        acts = jnp.zeros((NZ * ROWS, WIDTHS[q]), F32)
        for j in range(8):
            if j % 2 == 0:
                left_side = abuf[j // 4, :, :, (j % 4) * 256 : (j % 4) * 256 + 512]
            else:
                left_side = bbuf[:, j // 2]
            first = (j % 4) * 2
            right_side = wbufs[q][j // 4, first : first + 2].reshape(512, WIDTHS[q])
            acts = acts + jnp.dot(
                left_side.reshape(NZ * ROWS, 512), right_side, preferred_element_type=F32
            )
        return acts * scale

    def gated(gate, upper):
        value = gate / (1.0 + jnp.exp(-gate)) * upper
        return value.astype(BF16).reshape(NZ, ROWS, 128)

    owner = (z // 4) * 2 + x_lo
    stays = z // 4 == h

    def send_hidden(q):
        @pl.loop(1, NZ)
        def _(o):
            zz = (z + o) % NZ
            remote(
                hbuf.at[q, zz],
                hid_out.at[q, h, z % 4],
                send_sem.at[OUT + q],
                out_sem.at[q],
                place(owner, y, zz, c),
            ).start()

        @pl.when(stays)
        def _():
            pltpu.make_async_copy(hbuf.at[q, z], hid_out.at[q, h, z % 4], out_sem.at[q]).start()

        @pl.when(jnp.logical_not(stays))
        def _():
            remote(
                hbuf.at[q, z],
                hid_out.at[q, h, z % 4],
                send_sem.at[OUT + q],
                out_sem.at[q],
                to_across,
            ).start()

    core_wait(0)
    acts = product(0)
    hbuf[0, :, :, 0:128] = gated(acts[:, 0:128], acts[:, 128:256])
    core_wait(1)
    acts = product(1)
    hbuf[0, :, :, 128:256] = gated(acts[:, 0:128], acts[:, 128:256])
    send_hidden(0)
    stage_three(2)
    core_wait(2)
    acts = product(2)
    hbuf[1, :, :, 0:128] = gated(acts[:, 0:128], acts[:, 128:256])
    hbuf[1, :, :, 128:256] = gated(acts[:, 256:384], pltpu.roll(acts[:, 256:384], 64, 1))
    send_hidden(1)

    remote(mix_out.at[0], mix_out.at[0], send_sem.at[MIX], mix_sem, to_across).wait_recv()
    for q in range(2):
        whole = hid_out.at[q]
        remote(whole, whole, send_sem.at[OUT + q], out_sem.at[q], to_across).wait_recv()

    def sent(index, ref):
        remote(ref, ref, send_sem.at[index], mix_sem, to_across).wait_send()

    for q in range(CHUNKS):
        sent(A2A + q, sbufs[q].at[pl.ds(0, PLANE - 1)])
        for _ in range(2):
            sent(X1 + q, held(q, x))
        for _ in range(2):
            sent(X2 + q, held_half(q, left, 0))
        sent(CORE + q, wbufs[q].at[:, :, c])
    sent(RES, res.at[0])
    sent(RS, rsbuf.at[pl.ds(0, 7)])
    sent(GATHER, squares.at[pl.ds(0, 3)])
    sent(GATHER, ybuf.at[pl.ds(0, 3)])
    sent(MIX, ybuf.at[0])
    for chain in range(2):
        sent(RING + chain, abuf.at[chain, pl.ds(0, 7)])
    sent(RING + 2, bbuf.at[pl.ds(0, 7), 0])
    sent(SPREAD, abuf.at[:, pl.ds(0, 6)])
    for q in range(2):
        sent(OUT + q, hbuf.at[q, pl.ds(0, 7)])

    @pl.when(jnp.logical_not(stays))
    def _():
        for q in range(2):
            sent(OUT + q, hbuf.at[q, 0])

    store_g.wait()
    store_u.wait()
    store_mix.wait()


def finish(
    g_in, u_in, mix_in, hid_in, g_out, u_out, mix_out, hid_out, shards, mix32, hid32, sem
):
    halves = [pl.ds(0, FF // 2), pl.ds(FF // 2, FF // 2)]
    load, store = [], []
    for i, (source, dest) in enumerate(((g_in, g_out), (u_in, u_out))):
        for k, cols in enumerate(halves):
            held = shards.at[i, :, cols]
            load.append(pltpu.make_async_copy(source.at[:, cols], held, sem.at[2 * i + k]))
            store.append(pltpu.make_async_copy(held, dest.at[:, cols], sem.at[4 + 2 * i + k]))
    for copy in load:
        copy.start()
    lane = lax.broadcasted_iota(jnp.int32, (ROWS, 128), 1)
    for s in range(2):
        mix32[:, s, :] = mix_in[s].astype(F32)
        for p in range(2):
            even, odd = 2 * p, 2 * p + 1
            base = p * PAIR
            middle = jnp.where(
                lane < 64,
                hid_in[1, s, even, :, 128:256].astype(F32),
                hid_in[1, s, odd, :, 128:256].astype(F32),
            )
            hid32[:, s, base : base + 256] = hid_in[0, s, even].astype(F32)
            hid32[:, s, base + 256 : base + 384] = hid_in[1, s, even, :, 0:128].astype(F32)
            hid32[:, s, base + 384 : base + 512] = middle
            hid32[:, s, base + 512 : base + 768] = hid_in[0, s, odd].astype(F32)
            hid32[:, s, base + 768 : base + 896] = hid_in[1, s, odd, :, 0:128].astype(F32)
    for first, second in zip(load, store):
        first.wait()
        second.start()
    mix_out[...] = mix32[...].astype(BF16)
    hid_out[...] = hid32[...].astype(BF16)
    for copy in store:
        copy.wait()


def on_device(
    gate_param,
    up_param,
    gate_grad,
    up_grad,
    gate_mom,
    up_mom,
    gate_var,
    up_var,
    queries,
    new_keys,
    new_values,
    cache_keys,
    cache_values,
    cache_len,
    residual,
    out_proj,
    norm_gain,
):
    dma = pltpu.SemaphoreType.DMA
    vmem = pltpu.VMEM
    anywhere = pl.BlockSpec(memory_space=pl.ANY)
    inside = pl.BlockSpec(memory_space=vmem)
    shard = jax.ShapeDtypeStruct((16, FF), BF16)
    gate_updated, up_updated, mixed, hidden = pl.pallas_call(
        kernel,
        out_shape=(
            shard,
            shard,
            jax.ShapeDtypeStruct((2, ROWS, 512), BF16),
            jax.ShapeDtypeStruct((2, 2, 4, ROWS, 256), BF16),
        ),
        in_specs=[pl.BlockSpec(memory_space=pltpu.SMEM)] + [anywhere] * 16,
        out_specs=[anywhere] * 4,
        scratch_shapes=[
            vmem((8, 16, FF), BF16),
            vmem((16, FF), BF16),
            vmem((16, FF), BF16),
            *[vmem((PLANE, 16, width), BF16) for width in WIDTHS],
            *[vmem((2, NZ, 2, NY, 2, 16, width), BF16) for width in WIDTHS],
            vmem((2, ROWS, 2, 512), BF16),
            vmem((2, ROWS, 2, HD), BF16),
            vmem((2, ROWS, 2, 512), F32),
            vmem((ROWS, 16, HD), F32),
            vmem((ROWS, 8, HD), F32),
            vmem((2, ROWS, 512), BF16),
            vmem((ROWS, PADDED, HD), BF16),
            vmem((ROWS, PADDED, HD), BF16),
            vmem((512, D), BF16),
            vmem((D,), BF16),
            vmem((ROWS, 8, HD), F32),
            vmem((2 * ROWS, 512), BF16),
            vmem((8, 2, ROWS, 512), BF16),
            vmem((8, 2, ROWS, 512), BF16),
            vmem((2, ROWS, 512), BF16),
            vmem((8, ROWS, 512), BF16),
            vmem((NY, ROWS, 128), F32),
            vmem((2, NZ, ROWS, D // 4), BF16),
            vmem((NZ, NY, ROWS, 512), BF16),
            vmem((2, NZ, ROWS, 256), BF16),
            vmem((8, 1, 512), F32),
            dma((16,)),
            dma((22,)),
            dma((CHUNKS,)),
            dma((2 * CHUNKS,)),
            dma((2 * CHUNKS,)),
            dma((CHUNKS,)),
            dma(()),
            dma(()),
            dma(()),
            dma(()),
            dma((24,)),
            dma(()),
            dma(()),
            dma((2,)),
            dma((3,)),
        ],
        compiler_params=pltpu.CompilerParams(
            collective_id=0, has_side_effects=True, vmem_limit_bytes=56 * 1024 * 1024
        ),
    )(
        cache_len,
        gate_param, up_param, gate_grad, up_grad, gate_mom, up_mom, gate_var, up_var,
        queries, new_keys, new_values, cache_keys, cache_values, residual, out_proj, norm_gain,
    )
    return pl.pallas_call(
        finish,
        out_shape=(
            shard,
            shard,
            jax.ShapeDtypeStruct((ROWS, 2, 512), BF16),
            jax.ShapeDtypeStruct((ROWS, 2, 1792), BF16),
        ),
        in_specs=[anywhere, anywhere, inside, inside],
        out_specs=(anywhere, anywhere, inside, inside),
        scratch_shapes=[
            vmem((2, 16, FF), BF16),
            vmem((ROWS, 2, 512), F32),
            vmem((ROWS, 2, 1792), F32),
            dma((8,)),
        ],
        compiler_params=pltpu.CompilerParams(vmem_limit_bytes=56 * 1024 * 1024),
    )(gate_updated, up_updated, mixed, hidden)


def solution(mesh):
    both = P(("dp", "tp"), None)
    group = P("dp", None, "tp")
    return jax.shard_map(
        on_device,
        mesh=mesh,
        in_specs=(both,) * 8 + (group,) * 5 + (P("dp"), group, P("tp", None), P()),
        out_specs=(both, both, group, group),
        check_vma=False,
    )
```

```python
import functools
import math

import jax
import jax.numpy as jnp
from jax import lax
from jax.experimental import pallas as pl
from jax.experimental.pallas import tpu as pltpu
from jax.sharding import PartitionSpec as P

MESH = pl.DeviceIdType.MESH
F32 = jnp.float32
BF16 = jnp.bfloat16

HD = 128
ROWS = 32
SLOTS = 192
PADDED = 208
D = 4096
FF = 14336
NZ, NY = 8, 4
PLANE = NZ * NY
WIDTHS = (256, 256, 384)
CHUNKS = len(WIDTHS)
A2A, X1, X2, CORE, OUT = 0, 3, 6, 9, 12
RES, RS, GATHER, MIX, SPREAD, RING = range(14, 20)
PAIR = 896

beta_one = 0.9
beta_two = 0.95
adam_step = 20
learn_rate = 0.1
decay_rate = 0.1
epsilon_adam = 1e-08
epsilon_norm = 1e-05
masked_score = -1e30


def adamw_update(param, grad, moment, second):
    grad32 = grad.astype(F32)
    moment_new = beta_one * moment.astype(F32) + (1.0 - beta_one) * grad32
    second_new = beta_two * second.astype(F32) + (1.0 - beta_two) * grad32 * grad32
    corr_one = 1.0 - beta_one**adam_step
    corr_two = 1.0 - beta_two**adam_step
    direction = moment_new * (1.0 / corr_one) / (
        jnp.sqrt(second_new * (1.0 / corr_two)) + epsilon_adam
    )
    param32 = param.astype(F32)
    return param32 - learn_rate * (direction + decay_rate * param32)


def kernel(
    len_in,
    gp, up, gg, ug, gm, um, gv, uv,
    q_in, nk_in, nv_in, ck_in, cv_in, res_in, wo_in, gain_in,
    g_out, u_out, mix_out, hid_out,
    adam, gnew, unew, sbuf0, sbuf1, sbuf2, wbuf0, wbuf1, wbuf2,
    raw, new_raw, raw32, new32, q32, res, kbuf, vbuf, wo, gain,
    ctx32, ctxb, pbuf, rsbuf, rres, ybuf, squares, abuf, bbuf, hbuf, gains,
    load_sem, send_sem, a2a_sem, x1_sem, x2_sem, core_sem,
    rs_sem, res_sem, y_sem, square_sem, z_sem, spread_sem, mix_sem, out_sem, store_sem,
):
    dp = lax.axis_index("dp")
    tp = lax.axis_index("tp")
    x_lo = dp // 16
    z = (dp // 2) % NZ
    c = dp % 2
    y = tp // 2
    h = tp % 2
    x = h * 2 + x_lo
    other = 1 - h

    def place(xx, yy, zz, cc):
        return ((xx % 2) * 16 + zz * 2 + cc, yy * 2 + xx // 2)

    right = (x + 1) % 4
    left = (x + 3) % 4
    across = (x + 2) % 4
    z_up = (z + 1) % NZ
    z_dn = (z + NZ - 1) % NZ

    load_q = pltpu.make_async_copy(q_in, raw.at[0], load_sem.at[8])
    load_res = pltpu.make_async_copy(res_in, raw.at[1], load_sem.at[9])
    load_nk = pltpu.make_async_copy(nk_in, new_raw.at[0], load_sem.at[10])
    load_nv = pltpu.make_async_copy(nv_in, new_raw.at[1], load_sem.at[11])
    load_k = pltpu.make_async_copy(ck_in, kbuf.at[:, pl.ds(0, SLOTS), :], load_sem.at[12])
    load_v = pltpu.make_async_copy(cv_in, vbuf.at[:, pl.ds(0, SLOTS), :], load_sem.at[13])
    load_wo = pltpu.make_async_copy(wo_in, wo, load_sem.at[14])
    load_gain = pltpu.make_async_copy(gain_in, gain, load_sem.at[15])
    for copy in (load_q, load_res, load_nk, load_nv):
        copy.start()
    loads = []
    for i, ref in enumerate((gp, gg, gm, gv, up, ug, um, uv)):
        loads.append(pltpu.make_async_copy(ref, adam.at[i], load_sem.at[i]))
    for copy in loads:
        copy.start()
    for copy in (load_k, load_v, load_wo, load_gain):
        copy.start()

    barrier = pltpu.get_barrier_semaphore()

    def greet(where):
        pl.semaphore_signal(barrier, inc=1, device_id=where, device_id_type=MESH)

    @pl.loop(1, PLANE)
    def _(o):
        greet(place(x, (y + o // NZ) % NY, (z + o % NZ) % NZ, c))

    @pl.loop(1, NZ)
    def _(o):
        greet(place(across, y, (z + o) % NZ, c))

    @pl.loop(0, NY)
    def _(o):
        greet(place(across, (y + o) % NY, z, c))

    greet(place(right, y, z, c))
    greet(place(left, y, z, c))
    greet(place(x, y, z, 1 - c))

    for copy in (load_q, load_res, load_nk, load_nv):
        copy.wait()
    for i in range(2):
        raw32[i] = raw[i].astype(F32)
    for s in range(2):
        for g in range(4):
            q32[:, s * 4 + g, :] = raw32[0, :, s, g * HD : (g + 1) * HD]
        res[s] = raw32[1, :, s, :].astype(BF16)
    for i, buf in enumerate((kbuf, vbuf)):
        new32[...] = jnp.zeros_like(new32)
        new32[:, 0:2, :] = new_raw[i].astype(F32)
        buf[:, SLOTS:PADDED, :] = new32[...].astype(BF16)

    sbufs = (sbuf0, sbuf1, sbuf2)
    wbufs = (wbuf0, wbuf1, wbuf2)

    def remote(src, dst, send, recv, where):
        return pltpu.make_async_remote_copy(
            src_ref=src,
            dst_ref=dst,
            send_sem=send,
            recv_sem=recv,
            device_id=where,
            device_id_type=MESH,
        )

    for copy in loads:
        copy.wait()
    pl.semaphore_wait(barrier, PLANE - 1 + NZ - 1 + NY + 3)
    position = y * NZ + z

    def updated(start, width):
        cols = pl.ds(pl.multiple_of(start, 128), width)
        tiles = []
        for first, dest in ((0, gnew), (4, unew)):
            value = adamw_update(
                adam[first, :, cols],
                adam[first + 1, :, cols],
                adam[first + 2, :, cols],
                adam[first + 3, :, cols],
            )
            dest[:, cols] = value.astype(BF16)
            tiles.append([value[:, i * 128 : (i + 1) * 128] for i in range(width // 128)])
        return tiles

    def fill(dest, tiles):
        for i, tile in enumerate(tiles):
            dest[:, i * 128 : (i + 1) * 128] = tile.astype(BF16)

    def send_block(q, dest):
        remote(
            sbufs[q].at[dest],
            wbufs[q].at[x_lo, z, c, y, h],
            send_sem.at[A2A + q],
            a2a_sem.at[q],
            place(x, dest // NZ, dest % NZ, c),
        ).start()

    def first_chunks(dest):
        gate, upper = updated((dest // 2) * PAIR + (dest % 2) * 512, 256)
        fill(sbuf0.at[dest], (gate[0], upper[0]))
        fill(sbuf1.at[dest], (gate[1], upper[1]))

    @pl.loop(1, PLANE)
    def _(t):
        dest = (position + t) % PLANE
        first_chunks(dest)
        send_block(0, dest)

    @pl.loop(1, PLANE)
    def _(t):
        send_block(1, (position + t) % PLANE)

    first_chunks(position)
    wbuf0[x_lo, z, c, y, h] = sbuf0[position]
    wbuf1[x_lo, z, c, y, h] = sbuf1[position]

    def last_chunk(pair):
        gate, upper = updated(pair * PAIR + 256, 256)
        last_gate, last_upper = updated(pair * PAIR + 768, 128)
        lane = lax.broadcasted_iota(jnp.int32, (16, 128), 1)
        turned = pltpu.roll(upper[1], 64, 1)
        even = jnp.where(lane < 64, gate[1], turned)
        odd = jnp.where(lane < 64, turned, gate[1])
        fill(sbuf2.at[2 * pair], (gate[0], upper[0], even))
        fill(sbuf2.at[2 * pair + 1], (last_gate[0], last_upper[0], odd))

    to_across = place(across, y, z, c)
    res_copy = remote(res.at[other], rres.at[h], send_sem.at[RES], res_sem, to_across)
    res_copy.start()
    rres[h] = res[h]

    load_k.wait()
    load_v.wait()
    part = 8

    @pl.loop(0, ROWS // part)
    def _(i):
        rows = pl.ds(pl.multiple_of(i * part, part), part)
        slot = lax.broadcasted_iota(jnp.int32, (part, 8, PADDED), 2)
        token = lax.broadcasted_iota(jnp.int32, (part, 8, PADDED), 1) // 4
        scores = lax.dot_general(
            q32[rows].astype(BF16), kbuf[rows], (((2,), (2,)), ((0,), (0,))), preferred_element_type=F32
        ) * (1.0 / math.sqrt(HD))
        filled = jnp.concatenate(
            [jnp.full((1, 8, PADDED), len_in[i * part + k], jnp.int32) for k in range(part)], axis=0
        )
        fresh = (slot >= SLOTS) & (slot <= SLOTS + token)
        scores = jnp.where((slot < filled) | fresh, scores, masked_score)
        expo = jnp.exp(scores - jnp.max(scores, axis=-1, keepdims=True))
        weights = (expo / jnp.sum(expo, axis=-1, keepdims=True)).astype(BF16)
        context = lax.dot_general(
            weights, vbuf[rows], (((2,), (1,)), ((0,), (0,))), preferred_element_type=F32
        )
        ctx32[rows] = context

    for s in range(2):
        for g in range(4):
            ctxb[s * ROWS : (s + 1) * ROWS, g * HD : (g + 1) * HD] = ctx32[:, s * 4 + g, :].astype(BF16)

    def held(q, xx):
        return wbufs[q].at[xx % 2, :, c, :, xx // 2]

    def held_half(q, xx, half):
        return wbufs[q].at[xx % 2, pl.ds(half * 4, 4), c, :, xx // 2]

    def wait_a2a(q):
        some = sbufs[q].at[pl.ds(0, PLANE - 1)]
        remote(some, some, send_sem.at[A2A + q], a2a_sem.at[q], to_across).wait_recv()

    to_right = place(right, y, z, c)
    to_left = place(left, y, z, c)
    to_twin = place(x, y, z, 1 - c)

    def stage_one(q):
        mine = held(q, x)
        for side, where in enumerate((to_right, to_left)):
            remote(mine, mine, send_sem.at[X1 + q], x1_sem.at[2 * q + side], where).start()
        remote(mine, mine, send_sem.at[CORE + q], core_sem.at[q], to_twin).start()

    def stage_two(q):
        from_left, from_right = held(q, left), held(q, right)
        remote(from_left, from_left, send_sem.at[X1 + q], x1_sem.at[2 * q], to_right).wait_recv()
        half = held_half(q, left, 0)
        remote(half, half, send_sem.at[X2 + q], x2_sem.at[2 * q], to_right).start()
        remote(from_right, from_right, send_sem.at[X1 + q], x1_sem.at[2 * q + 1], to_left).wait_recv()
        half = held_half(q, right, 1)
        remote(half, half, send_sem.at[X2 + q], x2_sem.at[2 * q + 1], to_left).start()
        for part in (from_left, from_right):
            remote(part, part, send_sem.at[CORE + q], core_sem.at[q], to_twin).start()

    def stage_three(q):
        for side in range(2):
            half = held_half(q, across, side)
            remote(half, half, send_sem.at[X2 + q], x2_sem.at[2 * q + side], to_right).wait_recv()
        part = held(q, across)
        remote(part, part, send_sem.at[CORE + q], core_sem.at[q], to_twin).start()

    load_wo.wait()

    @pl.loop(0, 8)
    def _(j):
        cols = pl.ds(pl.multiple_of(j * 512, 512), 512)
        partial = jnp.dot(ctxb[...], wo[:, cols], preferred_element_type=F32).astype(BF16)
        pbuf[j, 0] = partial[:ROWS]
        pbuf[j, 1] = partial[ROWS:]

    @pl.loop(1, 8)
    def _(o):
        yy = (y + o // 2) % NY
        hh = (h + o) % 2
        remote(
            pbuf.at[pl.ds(2 * yy, 2), hh],
            rsbuf.at[tp],
            send_sem.at[RS],
            rs_sem,
            place(hh * 2 + x_lo, yy, z, c),
        ).start()

    rsbuf[tp] = pbuf[pl.ds(2 * y, 2), h]

    wait_a2a(0)
    stage_one(0)

    @pl.loop(1, 16)
    def _(t):
        pair = (position // 2 + t) % 16
        last_chunk(pair)
        send_block(2, 2 * pair)
        send_block(2, 2 * pair + 1)

    last_chunk(position // 2)
    send_block(2, position + 1 - 2 * (position % 2))
    wbuf2[x_lo, z, c, y, h] = sbuf2[position]
    store_g = pltpu.make_async_copy(gnew, g_out, store_sem.at[0])
    store_u = pltpu.make_async_copy(unew, u_out, store_sem.at[1])
    store_g.start()
    store_u.start()

    some = rsbuf.at[pl.ds(0, 7)]
    remote(some, some, send_sem.at[RS], rs_sem, to_across).wait_recv()
    remote(res.at[0], rres.at[0], send_sem.at[RES], res_sem, to_across).wait_recv()
    square = jnp.zeros((ROWS, 1), F32)
    for k in range(2):
        total = rsbuf[0, k].astype(F32)
        for i in range(1, 8):
            total = total + rsbuf[i, k].astype(F32)
        ybuf[2 * y + k] = (rres[k].astype(F32) + total).astype(BF16)
        value = ybuf[2 * y + k].astype(F32)
        square = square + jnp.sum(value * value, axis=-1, keepdims=True)
    squares[y] = jnp.broadcast_to(square, (ROWS, 128))

    y_peers = [place(x, (y + o) % NY, z, c) for o in range(1, NY)]
    for where in y_peers:
        remote(squares.at[y], squares.at[y], send_sem.at[GATHER], square_sem, where).start()
    for where in y_peers:
        mine = ybuf.at[2 * y]
        remote(mine, mine, send_sem.at[GATHER], y_sem, where).start()
    remote(ybuf.at[2 * y + other], mix_out.at[h], send_sem.at[MIX], mix_sem, to_across).start()
    store_mix = pltpu.make_async_copy(ybuf.at[2 * y + h], mix_out.at[h], store_sem.at[2])
    store_mix.start()
    wait_a2a(1)
    stage_one(1)
    load_gain.wait()
    gain32 = gain[...].astype(F32).reshape(1, D)
    for j in range(8):
        gains[j] = gain32[:, j * 512 : (j + 1) * 512]
    some = squares.at[pl.ds(0, 3)]
    remote(some, some, send_sem.at[GATHER], square_sem, to_across).wait_recv()
    square = (squares[0] + squares[1] + squares[2] + squares[3])[:, 0:1]
    factor = lax.rsqrt(square * (1.0 / D) + epsilon_norm)
    bbuf[z, y] = (ybuf[2 * y + 1].astype(F32) * factor * gains[2 * y + 1]).astype(BF16)

    to_up = place(x, y, z_up, c)
    to_dn = place(x, y, z_dn, c)

    def block(chain, shift):
        zz = (z + NZ + shift) % NZ
        return bbuf.at[zz, y] if chain == 2 else abuf.at[chain, zz]

    to_side = (to_up, to_dn)

    def ring_copy(chain, step, side, part):
        return remote(
            part, part, send_sem.at[RING + chain], z_sem.at[chain * 8 + step * 2 + side], to_side[side]
        )

    def ring_part(chain, step, side):
        part = block(chain, (-step, step)[side])
        return part.at[pl.ds(side * 16, 16)] if step == 3 else part

    def ring_send(chain, step, side):
        ring_copy(chain, step, side, ring_part(chain, step, side)).start()

    def ring_take(chain, step, side):
        shift = (-step - 1, step + 1)[side]
        part = block(chain, shift)
        if step == 3:
            part = part.at[pl.ds(side * 16, 16)]
        ring_copy(chain, step, side, part).wait_recv()

    def spread(shift):
        for where in y_peers:
            part = block(2, shift)
            remote(part, part, send_sem.at[SPREAD], spread_sem, where).start()

    def advance(chain, step):
        for side in range(2):
            ring_take(chain, step, side)
            if step < 3:
                ring_send(chain, step + 1, side)
        if chain == 2:
            if step < 3:
                spread(-step - 1)
                spread(step + 1)
            else:
                spread(4)

    for side in range(2):
        ring_send(2, 0, side)
    spread(0)
    some = ybuf.at[pl.ds(0, 3)]
    remote(some, some, send_sem.at[GATHER], y_sem, to_across).wait_recv()
    for chain in range(2):
        for k in range(2):
            j = 4 * chain + 2 * k
            abuf[chain, z, :, k * 512 : (k + 1) * 512] = (
                ybuf[j].astype(F32) * factor * gains[j]
            ).astype(BF16)
        for side in range(2):
            ring_send(chain, 0, side)
    stage_two(0)
    advance(2, 0)
    advance(0, 0)
    advance(1, 0)
    advance(2, 1)
    wait_a2a(2)
    stage_one(2)
    advance(0, 1)
    advance(1, 1)
    advance(2, 2)
    stage_two(1)
    advance(0, 2)
    advance(1, 2)
    advance(2, 3)
    stage_three(0)
    advance(0, 3)
    advance(1, 3)
    stage_two(2)
    stage_three(1)
    some = abuf.at[:, pl.ds(0, 6)]
    remote(some, some, send_sem.at[SPREAD], spread_sem, to_across).wait_recv()

    def core_wait(q):
        both = wbufs[q].at[:, :, 1 - c]
        remote(both, both, send_sem.at[CORE + q], core_sem.at[q], to_twin).wait_recv()

    scale = 1.0 / math.sqrt(D)

    def product(q):
        acts = jnp.zeros((NZ * ROWS, WIDTHS[q]), F32)
        for j in range(8):
            if j % 2 == 0:
                left_side = abuf[j // 4, :, :, (j % 4) * 256 : (j % 4) * 256 + 512]
            else:
                left_side = bbuf[:, j // 2]
            first = (j % 4) * 2
            right_side = wbufs[q][j // 4, first : first + 2].reshape(512, WIDTHS[q])
            acts = acts + jnp.dot(
                left_side.reshape(NZ * ROWS, 512), right_side, preferred_element_type=F32
            )
        return acts * scale

    def gated(gate, upper):
        value = gate / (1.0 + jnp.exp(-gate)) * upper
        return value.astype(BF16).reshape(NZ, ROWS, 128)

    owner = (z // 4) * 2 + x_lo
    stays = z // 4 == h

    def send_hidden(q):
        @pl.loop(1, NZ)
        def _(o):
            zz = (z + o) % NZ
            remote(
                hbuf.at[q, zz],
                hid_out.at[q, h, z % 4],
                send_sem.at[OUT + q],
                out_sem.at[q],
                place(owner, y, zz, c),
            ).start()

        @pl.when(stays)
        def _():
            pltpu.make_async_copy(hbuf.at[q, z], hid_out.at[q, h, z % 4], out_sem.at[q]).start()

        @pl.when(jnp.logical_not(stays))
        def _():
            remote(
                hbuf.at[q, z],
                hid_out.at[q, h, z % 4],
                send_sem.at[OUT + q],
                out_sem.at[q],
                to_across,
            ).start()

    core_wait(0)
    acts = product(0)
    hbuf[0, :, :, 0:128] = gated(acts[:, 0:128], acts[:, 128:256])
    core_wait(1)
    acts = product(1)
    hbuf[0, :, :, 128:256] = gated(acts[:, 0:128], acts[:, 128:256])
    send_hidden(0)
    stage_three(2)
    core_wait(2)
    acts = product(2)
    hbuf[1, :, :, 0:128] = gated(acts[:, 0:128], acts[:, 128:256])
    hbuf[1, :, :, 128:256] = gated(acts[:, 256:384], pltpu.roll(acts[:, 256:384], 64, 1))
    send_hidden(1)

    remote(mix_out.at[0], mix_out.at[0], send_sem.at[MIX], mix_sem, to_across).wait_recv()
    for q in range(2):
        whole = hid_out.at[q]
        remote(whole, whole, send_sem.at[OUT + q], out_sem.at[q], to_across).wait_recv()

    def sent(index, ref):
        remote(ref, ref, send_sem.at[index], mix_sem, to_across).wait_send()

    for q in range(CHUNKS):
        sent(A2A + q, sbufs[q].at[pl.ds(0, PLANE - 1)])
        for _ in range(2):
            sent(X1 + q, held(q, x))
        for _ in range(2):
            sent(X2 + q, held_half(q, left, 0))
        sent(CORE + q, wbufs[q].at[:, :, c])
    sent(RES, res.at[0])
    sent(RS, rsbuf.at[pl.ds(0, 7)])
    sent(GATHER, squares.at[pl.ds(0, 3)])
    sent(GATHER, ybuf.at[pl.ds(0, 3)])
    sent(MIX, ybuf.at[0])
    for chain in range(2):
        sent(RING + chain, abuf.at[chain, pl.ds(0, 7)])
    sent(RING + 2, bbuf.at[pl.ds(0, 7), 0])
    sent(SPREAD, abuf.at[:, pl.ds(0, 6)])
    for q in range(2):
        sent(OUT + q, hbuf.at[q, pl.ds(0, 7)])

    @pl.when(jnp.logical_not(stays))
    def _():
        for q in range(2):
            sent(OUT + q, hbuf.at[q, 0])

    store_g.wait()
    store_u.wait()
    store_mix.wait()


def finish(
    g_in, u_in, mix_hbm, hid_hbm, g_out, u_out, mix_out, hid_out,
    shards, mix_in, hid_in, mix32, hid32, sem,
):
    halves = [pl.ds(0, FF // 2), pl.ds(FF // 2, FF // 2)]
    load, store = [], []
    for i, (source, dest) in enumerate(((g_in, g_out), (u_in, u_out))):
        for k, cols in enumerate(halves):
            held = shards.at[i, :, cols]
            load.append(pltpu.make_async_copy(source.at[:, cols], held, sem.at[2 * i + k]))
            store.append(pltpu.make_async_copy(held, dest.at[:, cols], sem.at[4 + 2 * i + k]))
    load_hid = pltpu.make_async_copy(hid_hbm, hid_in, sem.at[8])
    load_mix = pltpu.make_async_copy(mix_hbm, mix_in, sem.at[9])
    load_hid.start()
    load_mix.start()
    for copy in load:
        copy.start()
    load_hid.wait()
    load_mix.wait()
    lane = lax.broadcasted_iota(jnp.int32, (ROWS, 128), 1)
    for s in range(2):
        mix32[:, s, :] = mix_in[s].astype(F32)
        for p in range(2):
            even, odd = 2 * p, 2 * p + 1
            base = p * PAIR
            middle = jnp.where(
                lane < 64,
                hid_in[1, s, even, :, 128:256].astype(F32),
                hid_in[1, s, odd, :, 128:256].astype(F32),
            )
            hid32[:, s, base : base + 256] = hid_in[0, s, even].astype(F32)
            hid32[:, s, base + 256 : base + 384] = hid_in[1, s, even, :, 0:128].astype(F32)
            hid32[:, s, base + 384 : base + 512] = middle
            hid32[:, s, base + 512 : base + 768] = hid_in[0, s, odd].astype(F32)
            hid32[:, s, base + 768 : base + 896] = hid_in[1, s, odd, :, 0:128].astype(F32)
    for first, second in zip(load, store):
        first.wait()
        second.start()
    mix_out[...] = mix32[...].astype(BF16)
    hid_out[...] = hid32[...].astype(BF16)
    for copy in store:
        copy.wait()


def on_device(
    gate_param,
    up_param,
    gate_grad,
    up_grad,
    gate_mom,
    up_mom,
    gate_var,
    up_var,
    queries,
    new_keys,
    new_values,
    cache_keys,
    cache_values,
    cache_len,
    residual,
    out_proj,
    norm_gain,
):
    dma = pltpu.SemaphoreType.DMA
    vmem = pltpu.VMEM
    anywhere = pl.BlockSpec(memory_space=pl.ANY)
    inside = pl.BlockSpec(memory_space=vmem)
    shard = jax.ShapeDtypeStruct((16, FF), BF16)
    gate_updated, up_updated, mixed, hidden = pl.pallas_call(
        kernel,
        out_shape=(
            shard,
            shard,
            jax.ShapeDtypeStruct((2, ROWS, 512), BF16),
            jax.ShapeDtypeStruct((2, 2, 4, ROWS, 256), BF16),
        ),
        in_specs=[pl.BlockSpec(memory_space=pltpu.SMEM)] + [anywhere] * 16,
        out_specs=[anywhere] * 4,
        scratch_shapes=[
            vmem((8, 16, FF), BF16),
            vmem((16, FF), BF16),
            vmem((16, FF), BF16),
            *[vmem((PLANE, 16, width), BF16) for width in WIDTHS],
            *[vmem((2, NZ, 2, NY, 2, 16, width), BF16) for width in WIDTHS],
            vmem((2, ROWS, 2, 512), BF16),
            vmem((2, ROWS, 2, HD), BF16),
            vmem((2, ROWS, 2, 512), F32),
            vmem((ROWS, 16, HD), F32),
            vmem((ROWS, 8, HD), F32),
            vmem((2, ROWS, 512), BF16),
            vmem((ROWS, PADDED, HD), BF16),
            vmem((ROWS, PADDED, HD), BF16),
            vmem((512, D), BF16),
            vmem((D,), BF16),
            vmem((ROWS, 8, HD), F32),
            vmem((2 * ROWS, 512), BF16),
            vmem((8, 2, ROWS, 512), BF16),
            vmem((8, 2, ROWS, 512), BF16),
            vmem((2, ROWS, 512), BF16),
            vmem((8, ROWS, 512), BF16),
            vmem((NY, ROWS, 128), F32),
            vmem((2, NZ, ROWS, D // 4), BF16),
            vmem((NZ, NY, ROWS, 512), BF16),
            vmem((2, NZ, ROWS, 256), BF16),
            vmem((8, 1, 512), F32),
            dma((16,)),
            dma((22,)),
            dma((CHUNKS,)),
            dma((2 * CHUNKS,)),
            dma((2 * CHUNKS,)),
            dma((CHUNKS,)),
            dma(()),
            dma(()),
            dma(()),
            dma(()),
            dma((24,)),
            dma(()),
            dma(()),
            dma((2,)),
            dma((3,)),
        ],
        compiler_params=pltpu.CompilerParams(
            collective_id=0, has_side_effects=True, vmem_limit_bytes=56 * 1024 * 1024
        ),
    )(
        cache_len,
        gate_param, up_param, gate_grad, up_grad, gate_mom, up_mom, gate_var, up_var,
        queries, new_keys, new_values, cache_keys, cache_values, residual, out_proj, norm_gain,
    )
    return pl.pallas_call(
        finish,
        out_shape=(
            shard,
            shard,
            jax.ShapeDtypeStruct((ROWS, 2, 512), BF16),
            jax.ShapeDtypeStruct((ROWS, 2, 1792), BF16),
        ),
        in_specs=[anywhere] * 4,
        out_specs=(anywhere, anywhere, inside, inside),
        scratch_shapes=[
            vmem((2, 16, FF), BF16),
            vmem((2, ROWS, 512), BF16),
            vmem((2, 2, 4, ROWS, 256), BF16),
            vmem((ROWS, 2, 512), F32),
            vmem((ROWS, 2, 1792), F32),
            dma((10,)),
        ],
        compiler_params=pltpu.CompilerParams(vmem_limit_bytes=56 * 1024 * 1024),
    )(gate_updated, up_updated, mixed, hidden)


def solution(mesh):
    both = P(("dp", "tp"), None)
    group = P("dp", None, "tp")
    return jax.shard_map(
        on_device,
        mesh=mesh,
        in_specs=(both,) * 8 + (group,) * 5 + (P("dp"), group, P("tp", None), P()),
        out_specs=(both, both, group, group),
        check_vma=False,
    )
```

```python
import functools
import math

import jax
import jax.numpy as jnp
from jax import lax
from jax.experimental import pallas as pl
from jax.experimental.pallas import tpu as pltpu
from jax.sharding import PartitionSpec as P

MESH = pl.DeviceIdType.MESH
F32 = jnp.float32
BF16 = jnp.bfloat16

HD = 128
ROWS = 32
SLOTS = 192
PADDED = 208
D = 4096
FF = 14336
NZ, NY = 8, 4
PLANE = NZ * NY
WIDTHS = (256, 256, 384)
CHUNKS = len(WIDTHS)
A2A, X1, X2, CORE, OUT = 0, 3, 6, 9, 12
RES, RS, GATHER, MIX, SPREAD, RING = range(14, 20)
PAIR = 896

beta_one = 0.9
beta_two = 0.95
adam_step = 20
learn_rate = 0.1
decay_rate = 0.1
epsilon_adam = 1e-08
epsilon_norm = 1e-05
masked_score = -1e30


def adamw_update(param, grad, moment, second):
    grad32 = grad.astype(F32)
    moment_new = beta_one * moment.astype(F32) + (1.0 - beta_one) * grad32
    second_new = beta_two * second.astype(F32) + (1.0 - beta_two) * grad32 * grad32
    corr_one = 1.0 - beta_one**adam_step
    corr_two = 1.0 - beta_two**adam_step
    direction = moment_new * (1.0 / corr_one) / (
        jnp.sqrt(second_new * (1.0 / corr_two)) + epsilon_adam
    )
    param32 = param.astype(F32)
    return param32 - learn_rate * (direction + decay_rate * param32)


def kernel(
    len_in,
    gp, up, gg, ug, gm, um, gv, uv,
    q_in, nk_in, nv_in, ck_in, cv_in, res_in, wo_in, gain_in,
    g_out, u_out, mix_out, hid_out,
    adam, gnew, unew, sbuf0, sbuf1, sbuf2, wbuf0, wbuf1, wbuf2,
    raw, new_raw, raw32, new32, q32, res, kbuf, vbuf, wo, gain,
    ctx32, ctxb, pbuf, rsbuf, rres, ybuf, squares, abuf, bbuf, hbuf, gains,
    load_sem, send_sem, a2a_sem, x1_sem, x2_sem, core_sem,
    rs_sem, res_sem, y_sem, square_sem, z_sem, spread_sem, mix_sem, out_sem, store_sem,
):
    dp = lax.axis_index("dp")
    tp = lax.axis_index("tp")
    x_lo = dp // 16
    z = (dp // 2) % NZ
    c = dp % 2
    y = tp // 2
    h = tp % 2
    x = h * 2 + x_lo
    other = 1 - h

    def place(xx, yy, zz, cc):
        return ((xx % 2) * 16 + zz * 2 + cc, yy * 2 + xx // 2)

    right = (x + 1) % 4
    left = (x + 3) % 4
    across = (x + 2) % 4
    z_up = (z + 1) % NZ
    z_dn = (z + NZ - 1) % NZ

    load_q = pltpu.make_async_copy(q_in, raw.at[0], load_sem.at[8])
    load_res = pltpu.make_async_copy(res_in, raw.at[1], load_sem.at[9])
    load_nk = pltpu.make_async_copy(nk_in, new_raw.at[0], load_sem.at[10])
    load_nv = pltpu.make_async_copy(nv_in, new_raw.at[1], load_sem.at[11])
    load_k = pltpu.make_async_copy(ck_in, kbuf.at[:, pl.ds(0, SLOTS), :], load_sem.at[12])
    load_v = pltpu.make_async_copy(cv_in, vbuf.at[:, pl.ds(0, SLOTS), :], load_sem.at[13])
    load_wo = pltpu.make_async_copy(wo_in, wo, load_sem.at[14])
    load_gain = pltpu.make_async_copy(gain_in, gain, load_sem.at[15])
    for copy in (load_q, load_res, load_nk, load_nv):
        copy.start()
    loads = []
    for i, ref in enumerate((gp, gg, gm, gv, up, ug, um, uv)):
        loads.append(pltpu.make_async_copy(ref, adam.at[i], load_sem.at[i]))
    for copy in loads:
        copy.start()
    for copy in (load_k, load_v, load_wo, load_gain):
        copy.start()

    barrier = pltpu.get_barrier_semaphore()

    def greet(where):
        pl.semaphore_signal(barrier, inc=1, device_id=where, device_id_type=MESH)

    @pl.loop(1, PLANE)
    def _(o):
        greet(place(x, (y + o // NZ) % NY, (z + o % NZ) % NZ, c))

    @pl.loop(1, NZ)
    def _(o):
        greet(place(across, y, (z + o) % NZ, c))

    @pl.loop(0, NY)
    def _(o):
        greet(place(across, (y + o) % NY, z, c))

    greet(place(right, y, z, c))
    greet(place(left, y, z, c))
    greet(place(x, y, z, 1 - c))

    for copy in (load_q, load_res, load_nk, load_nv):
        copy.wait()
    for i in range(2):
        raw32[i] = raw[i].astype(F32)
    for s in range(2):
        for g in range(4):
            q32[:, s * 4 + g, :] = raw32[0, :, s, g * HD : (g + 1) * HD]
        res[s] = raw32[1, :, s, :].astype(BF16)
    for i, buf in enumerate((kbuf, vbuf)):
        new32[...] = jnp.zeros_like(new32)
        new32[:, 0:2, :] = new_raw[i].astype(F32)
        buf[:, SLOTS:PADDED, :] = new32[...].astype(BF16)

    sbufs = (sbuf0, sbuf1, sbuf2)
    wbufs = (wbuf0, wbuf1, wbuf2)

    def remote(src, dst, send, recv, where):
        return pltpu.make_async_remote_copy(
            src_ref=src,
            dst_ref=dst,
            send_sem=send,
            recv_sem=recv,
            device_id=where,
            device_id_type=MESH,
        )

    for copy in loads:
        copy.wait()
    pl.semaphore_wait(barrier, PLANE - 1 + NZ - 1 + NY + 3)
    position = y * NZ + z

    def updated(start, width):
        cols = pl.ds(pl.multiple_of(start, 128), width)
        tiles = []
        for first, dest in ((0, gnew), (4, unew)):
            value = adamw_update(
                adam[first, :, cols],
                adam[first + 1, :, cols],
                adam[first + 2, :, cols],
                adam[first + 3, :, cols],
            )
            dest[:, cols] = value.astype(BF16)
            tiles.append([value[:, i * 128 : (i + 1) * 128] for i in range(width // 128)])
        return tiles

    def fill(dest, tiles):
        for i, tile in enumerate(tiles):
            dest[:, i * 128 : (i + 1) * 128] = tile.astype(BF16)

    def send_block(q, dest):
        remote(
            sbufs[q].at[dest],
            wbufs[q].at[x_lo, z, c, y, h],
            send_sem.at[A2A + q],
            a2a_sem.at[q],
            place(x, dest // NZ, dest % NZ, c),
        ).start()

    def early_chunk(q, dest):
        gate, upper = updated((dest // 2) * PAIR + (dest % 2) * 512 + q * 128, 128)
        fill(sbufs[q].at[dest], (gate[0], upper[0]))

    for q in range(2):
        @pl.loop(1, PLANE)
        def _(t, q=q):
            dest = (position + t) % PLANE
            early_chunk(q, dest)
            send_block(q, dest)

        early_chunk(q, position)
        wbufs[q][x_lo, z, c, y, h] = sbufs[q][position]

    def last_chunk(pair):
        gate, upper = updated(pair * PAIR + 256, 256)
        last_gate, last_upper = updated(pair * PAIR + 768, 128)
        lane = lax.broadcasted_iota(jnp.int32, (16, 128), 1)
        turned = pltpu.roll(upper[1], 64, 1)
        even = jnp.where(lane < 64, gate[1], turned)
        odd = jnp.where(lane < 64, turned, gate[1])
        fill(sbuf2.at[2 * pair], (gate[0], upper[0], even))
        fill(sbuf2.at[2 * pair + 1], (last_gate[0], last_upper[0], odd))

    to_across = place(across, y, z, c)
    res_copy = remote(res.at[other], rres.at[h], send_sem.at[RES], res_sem, to_across)
    res_copy.start()
    rres[h] = res[h]

    load_k.wait()
    load_v.wait()
    part = 8

    @pl.loop(0, ROWS // part)
    def _(i):
        rows = pl.ds(pl.multiple_of(i * part, part), part)
        slot = lax.broadcasted_iota(jnp.int32, (part, 8, PADDED), 2)
        token = lax.broadcasted_iota(jnp.int32, (part, 8, PADDED), 1) // 4
        scores = lax.dot_general(
            q32[rows].astype(BF16), kbuf[rows], (((2,), (2,)), ((0,), (0,))), preferred_element_type=F32
        ) * (1.0 / math.sqrt(HD))
        filled = jnp.concatenate(
            [jnp.full((1, 8, PADDED), len_in[i * part + k], jnp.int32) for k in range(part)], axis=0
        )
        fresh = (slot >= SLOTS) & (slot <= SLOTS + token)
        scores = jnp.where((slot < filled) | fresh, scores, masked_score)
        expo = jnp.exp(scores - jnp.max(scores, axis=-1, keepdims=True))
        weights = (expo / jnp.sum(expo, axis=-1, keepdims=True)).astype(BF16)
        context = lax.dot_general(
            weights, vbuf[rows], (((2,), (1,)), ((0,), (0,))), preferred_element_type=F32
        )
        ctx32[rows] = context

    for s in range(2):
        for g in range(4):
            ctxb[s * ROWS : (s + 1) * ROWS, g * HD : (g + 1) * HD] = ctx32[:, s * 4 + g, :].astype(BF16)

    def held(q, xx):
        return wbufs[q].at[xx % 2, :, c, :, xx // 2]

    def held_half(q, xx, half):
        return wbufs[q].at[xx % 2, pl.ds(half * 4, 4), c, :, xx // 2]

    def wait_a2a(q):
        some = sbufs[q].at[pl.ds(0, PLANE - 1)]
        remote(some, some, send_sem.at[A2A + q], a2a_sem.at[q], to_across).wait_recv()

    to_right = place(right, y, z, c)
    to_left = place(left, y, z, c)
    to_twin = place(x, y, z, 1 - c)

    def stage_one(q):
        mine = held(q, x)
        for side, where in enumerate((to_right, to_left)):
            remote(mine, mine, send_sem.at[X1 + q], x1_sem.at[2 * q + side], where).start()
        remote(mine, mine, send_sem.at[CORE + q], core_sem.at[q], to_twin).start()

    def stage_two(q):
        from_left, from_right = held(q, left), held(q, right)
        remote(from_left, from_left, send_sem.at[X1 + q], x1_sem.at[2 * q], to_right).wait_recv()
        half = held_half(q, left, 0)
        remote(half, half, send_sem.at[X2 + q], x2_sem.at[2 * q], to_right).start()
        remote(from_right, from_right, send_sem.at[X1 + q], x1_sem.at[2 * q + 1], to_left).wait_recv()
        half = held_half(q, right, 1)
        remote(half, half, send_sem.at[X2 + q], x2_sem.at[2 * q + 1], to_left).start()
        for part in (from_left, from_right):
            remote(part, part, send_sem.at[CORE + q], core_sem.at[q], to_twin).start()

    def stage_three(q):
        for side in range(2):
            half = held_half(q, across, side)
            remote(half, half, send_sem.at[X2 + q], x2_sem.at[2 * q + side], to_right).wait_recv()
        part = held(q, across)
        remote(part, part, send_sem.at[CORE + q], core_sem.at[q], to_twin).start()

    load_wo.wait()

    @pl.loop(0, 8)
    def _(j):
        cols = pl.ds(pl.multiple_of(j * 512, 512), 512)
        partial = jnp.dot(ctxb[...], wo[:, cols], preferred_element_type=F32).astype(BF16)
        pbuf[j, 0] = partial[:ROWS]
        pbuf[j, 1] = partial[ROWS:]

    @pl.loop(1, 8)
    def _(o):
        yy = (y + o // 2) % NY
        hh = (h + o) % 2
        remote(
            pbuf.at[pl.ds(2 * yy, 2), hh],
            rsbuf.at[tp],
            send_sem.at[RS],
            rs_sem,
            place(hh * 2 + x_lo, yy, z, c),
        ).start()

    rsbuf[tp] = pbuf[pl.ds(2 * y, 2), h]

    wait_a2a(0)
    stage_one(0)

    @pl.loop(1, 16)
    def _(t):
        pair = (position // 2 + t) % 16
        last_chunk(pair)
        send_block(2, 2 * pair)
        send_block(2, 2 * pair + 1)

    last_chunk(position // 2)
    send_block(2, position + 1 - 2 * (position % 2))
    wbuf2[x_lo, z, c, y, h] = sbuf2[position]
    store_g = pltpu.make_async_copy(gnew, g_out, store_sem.at[0])
    store_u = pltpu.make_async_copy(unew, u_out, store_sem.at[1])
    store_g.start()
    store_u.start()

    some = rsbuf.at[pl.ds(0, 7)]
    remote(some, some, send_sem.at[RS], rs_sem, to_across).wait_recv()
    remote(res.at[0], rres.at[0], send_sem.at[RES], res_sem, to_across).wait_recv()
    square = jnp.zeros((ROWS, 1), F32)
    for k in range(2):
        total = rsbuf[0, k].astype(F32)
        for i in range(1, 8):
            total = total + rsbuf[i, k].astype(F32)
        ybuf[2 * y + k] = (rres[k].astype(F32) + total).astype(BF16)
        value = ybuf[2 * y + k].astype(F32)
        square = square + jnp.sum(value * value, axis=-1, keepdims=True)
    squares[y] = jnp.broadcast_to(square, (ROWS, 128))

    y_peers = [place(x, (y + o) % NY, z, c) for o in range(1, NY)]
    for where in y_peers:
        remote(squares.at[y], squares.at[y], send_sem.at[GATHER], square_sem, where).start()
    for where in y_peers:
        mine = ybuf.at[2 * y]
        remote(mine, mine, send_sem.at[GATHER], y_sem, where).start()
    remote(ybuf.at[2 * y + other], mix_out.at[h], send_sem.at[MIX], mix_sem, to_across).start()
    store_mix = pltpu.make_async_copy(ybuf.at[2 * y + h], mix_out.at[h], store_sem.at[2])
    store_mix.start()
    wait_a2a(1)
    stage_one(1)
    load_gain.wait()
    gain32 = gain[...].astype(F32).reshape(1, D)
    for j in range(8):
        gains[j] = gain32[:, j * 512 : (j + 1) * 512]
    some = squares.at[pl.ds(0, 3)]
    remote(some, some, send_sem.at[GATHER], square_sem, to_across).wait_recv()
    square = (squares[0] + squares[1] + squares[2] + squares[3])[:, 0:1]
    factor = lax.rsqrt(square * (1.0 / D) + epsilon_norm)
    bbuf[z, y] = (ybuf[2 * y + 1].astype(F32) * factor * gains[2 * y + 1]).astype(BF16)

    to_up = place(x, y, z_up, c)
    to_dn = place(x, y, z_dn, c)

    def block(chain, shift):
        zz = (z + NZ + shift) % NZ
        return bbuf.at[zz, y] if chain == 2 else abuf.at[chain, zz]

    to_side = (to_up, to_dn)

    def ring_copy(chain, step, side, part):
        return remote(
            part, part, send_sem.at[RING + chain], z_sem.at[chain * 8 + step * 2 + side], to_side[side]
        )

    def ring_part(chain, step, side):
        part = block(chain, (-step, step)[side])
        return part.at[pl.ds(side * 16, 16)] if step == 3 else part

    def ring_send(chain, step, side):
        ring_copy(chain, step, side, ring_part(chain, step, side)).start()

    def ring_take(chain, step, side):
        shift = (-step - 1, step + 1)[side]
        part = block(chain, shift)
        if step == 3:
            part = part.at[pl.ds(side * 16, 16)]
        ring_copy(chain, step, side, part).wait_recv()

    def spread(shift):
        for where in y_peers:
            part = block(2, shift)
            remote(part, part, send_sem.at[SPREAD], spread_sem, where).start()

    def advance(chain, step):
        for side in range(2):
            ring_take(chain, step, side)
            if step < 3:
                ring_send(chain, step + 1, side)
        if chain == 2:
            if step < 3:
                spread(-step - 1)
                spread(step + 1)
            else:
                spread(4)

    for side in range(2):
        ring_send(2, 0, side)
    spread(0)
    some = ybuf.at[pl.ds(0, 3)]
    remote(some, some, send_sem.at[GATHER], y_sem, to_across).wait_recv()
    for chain in range(2):
        for k in range(2):
            j = 4 * chain + 2 * k
            abuf[chain, z, :, k * 512 : (k + 1) * 512] = (
                ybuf[j].astype(F32) * factor * gains[j]
            ).astype(BF16)
        for side in range(2):
            ring_send(chain, 0, side)
    stage_two(0)
    advance(2, 0)
    advance(0, 0)
    advance(1, 0)
    advance(2, 1)
    wait_a2a(2)
    stage_one(2)
    advance(0, 1)
    advance(1, 1)
    advance(2, 2)
    stage_two(1)
    advance(0, 2)
    advance(1, 2)
    advance(2, 3)
    stage_three(0)
    advance(0, 3)
    advance(1, 3)
    stage_two(2)
    stage_three(1)
    some = abuf.at[:, pl.ds(0, 6)]
    remote(some, some, send_sem.at[SPREAD], spread_sem, to_across).wait_recv()

    def core_wait(q):
        both = wbufs[q].at[:, :, 1 - c]
        remote(both, both, send_sem.at[CORE + q], core_sem.at[q], to_twin).wait_recv()

    scale = 1.0 / math.sqrt(D)

    def product(q):
        acts = jnp.zeros((NZ * ROWS, WIDTHS[q]), F32)
        for j in range(8):
            if j % 2 == 0:
                left_side = abuf[j // 4, :, :, (j % 4) * 256 : (j % 4) * 256 + 512]
            else:
                left_side = bbuf[:, j // 2]
            first = (j % 4) * 2
            right_side = wbufs[q][j // 4, first : first + 2].reshape(512, WIDTHS[q])
            acts = acts + jnp.dot(
                left_side.reshape(NZ * ROWS, 512), right_side, preferred_element_type=F32
            )
        return acts * scale

    def gated(gate, upper):
        value = gate / (1.0 + jnp.exp(-gate)) * upper
        return value.astype(BF16).reshape(NZ, ROWS, 128)

    owner = (z // 4) * 2 + x_lo
    stays = z // 4 == h

    def send_hidden(q):
        @pl.loop(1, NZ)
        def _(o):
            zz = (z + o) % NZ
            remote(
                hbuf.at[q, zz],
                hid_out.at[q, h, z % 4],
                send_sem.at[OUT + q],
                out_sem.at[q],
                place(owner, y, zz, c),
            ).start()

        @pl.when(stays)
        def _():
            pltpu.make_async_copy(hbuf.at[q, z], hid_out.at[q, h, z % 4], out_sem.at[q]).start()

        @pl.when(jnp.logical_not(stays))
        def _():
            remote(
                hbuf.at[q, z],
                hid_out.at[q, h, z % 4],
                send_sem.at[OUT + q],
                out_sem.at[q],
                to_across,
            ).start()

    core_wait(0)
    acts = product(0)
    hbuf[0, :, :, 0:128] = gated(acts[:, 0:128], acts[:, 128:256])
    core_wait(1)
    acts = product(1)
    hbuf[0, :, :, 128:256] = gated(acts[:, 0:128], acts[:, 128:256])
    send_hidden(0)
    stage_three(2)
    core_wait(2)
    acts = product(2)
    hbuf[1, :, :, 0:128] = gated(acts[:, 0:128], acts[:, 128:256])
    hbuf[1, :, :, 128:256] = gated(acts[:, 256:384], pltpu.roll(acts[:, 256:384], 64, 1))
    send_hidden(1)

    remote(mix_out.at[0], mix_out.at[0], send_sem.at[MIX], mix_sem, to_across).wait_recv()
    for q in range(2):
        whole = hid_out.at[q]
        remote(whole, whole, send_sem.at[OUT + q], out_sem.at[q], to_across).wait_recv()

    def sent(index, ref):
        remote(ref, ref, send_sem.at[index], mix_sem, to_across).wait_send()

    for q in range(CHUNKS):
        sent(A2A + q, sbufs[q].at[pl.ds(0, PLANE - 1)])
        for _ in range(2):
            sent(X1 + q, held(q, x))
        for _ in range(2):
            sent(X2 + q, held_half(q, left, 0))
        sent(CORE + q, wbufs[q].at[:, :, c])
    sent(RES, res.at[0])
    sent(RS, rsbuf.at[pl.ds(0, 7)])
    sent(GATHER, squares.at[pl.ds(0, 3)])
    sent(GATHER, ybuf.at[pl.ds(0, 3)])
    sent(MIX, ybuf.at[0])
    for chain in range(2):
        sent(RING + chain, abuf.at[chain, pl.ds(0, 7)])
    sent(RING + 2, bbuf.at[pl.ds(0, 7), 0])
    sent(SPREAD, abuf.at[:, pl.ds(0, 6)])
    for q in range(2):
        sent(OUT + q, hbuf.at[q, pl.ds(0, 7)])

    @pl.when(jnp.logical_not(stays))
    def _():
        for q in range(2):
            sent(OUT + q, hbuf.at[q, 0])

    store_g.wait()
    store_u.wait()
    store_mix.wait()


def finish(
    g_in, u_in, mix_hbm, hid_hbm, g_out, u_out, mix_out, hid_out,
    shards, mix_in, hid_in, mix32, hid32, sem,
):
    halves = [pl.ds(0, FF // 2), pl.ds(FF // 2, FF // 2)]
    load, store = [], []
    for i, (source, dest) in enumerate(((g_in, g_out), (u_in, u_out))):
        for k, cols in enumerate(halves):
            held = shards.at[i, :, cols]
            load.append(pltpu.make_async_copy(source.at[:, cols], held, sem.at[2 * i + k]))
            store.append(pltpu.make_async_copy(held, dest.at[:, cols], sem.at[4 + 2 * i + k]))
    load_hid = pltpu.make_async_copy(hid_hbm, hid_in, sem.at[8])
    load_mix = pltpu.make_async_copy(mix_hbm, mix_in, sem.at[9])
    load_hid.start()
    load_mix.start()
    for copy in load:
        copy.start()
    load_hid.wait()
    load_mix.wait()
    lane = lax.broadcasted_iota(jnp.int32, (ROWS, 128), 1)
    for s in range(2):
        mix32[:, s, :] = mix_in[s].astype(F32)
        for p in range(2):
            even, odd = 2 * p, 2 * p + 1
            base = p * PAIR
            middle = jnp.where(
                lane < 64,
                hid_in[1, s, even, :, 128:256].astype(F32),
                hid_in[1, s, odd, :, 128:256].astype(F32),
            )
            hid32[:, s, base : base + 256] = hid_in[0, s, even].astype(F32)
            hid32[:, s, base + 256 : base + 384] = hid_in[1, s, even, :, 0:128].astype(F32)
            hid32[:, s, base + 384 : base + 512] = middle
            hid32[:, s, base + 512 : base + 768] = hid_in[0, s, odd].astype(F32)
            hid32[:, s, base + 768 : base + 896] = hid_in[1, s, odd, :, 0:128].astype(F32)
    for first, second in zip(load, store):
        first.wait()
        second.start()
    mix_out[...] = mix32[...].astype(BF16)
    hid_out[...] = hid32[...].astype(BF16)
    for copy in store:
        copy.wait()


def on_device(
    gate_param,
    up_param,
    gate_grad,
    up_grad,
    gate_mom,
    up_mom,
    gate_var,
    up_var,
    queries,
    new_keys,
    new_values,
    cache_keys,
    cache_values,
    cache_len,
    residual,
    out_proj,
    norm_gain,
):
    dma = pltpu.SemaphoreType.DMA
    vmem = pltpu.VMEM
    anywhere = pl.BlockSpec(memory_space=pl.ANY)
    inside = pl.BlockSpec(memory_space=vmem)
    shard = jax.ShapeDtypeStruct((16, FF), BF16)
    gate_updated, up_updated, mixed, hidden = pl.pallas_call(
        kernel,
        out_shape=(
            shard,
            shard,
            jax.ShapeDtypeStruct((2, ROWS, 512), BF16),
            jax.ShapeDtypeStruct((2, 2, 4, ROWS, 256), BF16),
        ),
        in_specs=[pl.BlockSpec(memory_space=pltpu.SMEM)] + [anywhere] * 16,
        out_specs=[anywhere] * 4,
        scratch_shapes=[
            vmem((8, 16, FF), BF16),
            vmem((16, FF), BF16),
            vmem((16, FF), BF16),
            *[vmem((PLANE, 16, width), BF16) for width in WIDTHS],
            *[vmem((2, NZ, 2, NY, 2, 16, width), BF16) for width in WIDTHS],
            vmem((2, ROWS, 2, 512), BF16),
            vmem((2, ROWS, 2, HD), BF16),
            vmem((2, ROWS, 2, 512), F32),
            vmem((ROWS, 16, HD), F32),
            vmem((ROWS, 8, HD), F32),
            vmem((2, ROWS, 512), BF16),
            vmem((ROWS, PADDED, HD), BF16),
            vmem((ROWS, PADDED, HD), BF16),
            vmem((512, D), BF16),
            vmem((D,), BF16),
            vmem((ROWS, 8, HD), F32),
            vmem((2 * ROWS, 512), BF16),
            vmem((8, 2, ROWS, 512), BF16),
            vmem((8, 2, ROWS, 512), BF16),
            vmem((2, ROWS, 512), BF16),
            vmem((8, ROWS, 512), BF16),
            vmem((NY, ROWS, 128), F32),
            vmem((2, NZ, ROWS, D // 4), BF16),
            vmem((NZ, NY, ROWS, 512), BF16),
            vmem((2, NZ, ROWS, 256), BF16),
            vmem((8, 1, 512), F32),
            dma((16,)),
            dma((22,)),
            dma((CHUNKS,)),
            dma((2 * CHUNKS,)),
            dma((2 * CHUNKS,)),
            dma((CHUNKS,)),
            dma(()),
            dma(()),
            dma(()),
            dma(()),
            dma((24,)),
            dma(()),
            dma(()),
            dma((2,)),
            dma((3,)),
        ],
        compiler_params=pltpu.CompilerParams(
            collective_id=0, has_side_effects=True, vmem_limit_bytes=56 * 1024 * 1024
        ),
    )(
        cache_len,
        gate_param, up_param, gate_grad, up_grad, gate_mom, up_mom, gate_var, up_var,
        queries, new_keys, new_values, cache_keys, cache_values, residual, out_proj, norm_gain,
    )
    return pl.pallas_call(
        finish,
        out_shape=(
            shard,
            shard,
            jax.ShapeDtypeStruct((ROWS, 2, 512), BF16),
            jax.ShapeDtypeStruct((ROWS, 2, 1792), BF16),
        ),
        in_specs=[anywhere] * 4,
        out_specs=(anywhere, anywhere, inside, inside),
        scratch_shapes=[
            vmem((2, 16, FF), BF16),
            vmem((2, ROWS, 512), BF16),
            vmem((2, 2, 4, ROWS, 256), BF16),
            vmem((ROWS, 2, 512), F32),
            vmem((ROWS, 2, 1792), F32),
            dma((10,)),
        ],
        compiler_params=pltpu.CompilerParams(vmem_limit_bytes=56 * 1024 * 1024),
    )(gate_updated, up_updated, mixed, hidden)


def solution(mesh):
    both = P(("dp", "tp"), None)
    group = P("dp", None, "tp")
    return jax.shard_map(
        on_device,
        mesh=mesh,
        in_specs=(both,) * 8 + (group,) * 5 + (P("dp"), group, P("tp", None), P()),
        out_specs=(both, both, group, group),
        check_vma=False,
    )
```
